32 devices in a mesh: leaf: 4 (over z), trunk: 8 (over y, x, core).
Axes of the slice: x: 2, y: 2, z: 4, core: 2. Of those that a mesh axis runs over, the one named last changes fastest.
Arguments:
- trunk_tokens: bfloat16 [8, 2048, 1024], P('leaf', 'trunk'), may hold values from -6 to 6
- branch_tokens: bfloat16 [128, 128, 1024], P(('leaf', 'trunk')), may hold values from -6 to 6
- fork_offset: int32 [4, 8, 4], P('leaf', 'trunk'), may hold values from 0 to 255
- fork_tree: int32 [4, 8, 4], P('leaf', 'trunk'), may hold values from 0 to 1
- branch_len: int32 [128], P(('leaf', 'trunk')), may hold values from 0 to 128, as said below
- w_query: bfloat16 [1024, 1024], P('trunk'), may hold values from -0.1875 to 0.1875
- w_key: bfloat16 [1024, 1024], P('trunk'), may hold values from -0.1875 to 0.1875
- w_value: bfloat16 [1024, 1024], P('trunk'), may hold values from -0.1875 to 0.1875
- w_out: bfloat16 [1024, 1024], P('trunk'), may hold values from -0.1875 to 0.1875
Outputs:
- mixed: bfloat16 [128, 128, 1024], P(('leaf', 'trunk'))
The draws below stay inside these ranges and needn't reach their ends.
Inputs may be any that keep to these rules, and one draw needn't show every extreme that they name: `branch_len`: each length is a multiple of 128; some slot has the full 128 in every draw.
All inputs are finite; a program needn't handle non-finite values.
Results may differ from the reference program's by a relative error of at most 0.0065.
Values may be sent and summed in bfloat16 or wider, within the bound.
No kernel may reach another device: no remote copies, remote signals or barrier semaphores. Data moves between devices by JAX's collectives and lax.ppermute only.
A program may use at most 128 MiB of HBM per device.

```python
import jax
import jax.numpy as jnp
from jax import lax

D = 1024
H = 8
DH = 128
HD = 1024
TRUNK_TOK = 256
TREES_DEV = 2
CAP = 1
BLEN = 128
SLOTS = 4
TREES = 8
TRUNK_LEN = 2048
BRANCHES = 128
N_LEAF = 4
N_TRUNK = 8


def draw_branch_len(key, part):
    key_keep = jax.random.fold_in(key, 11)
    key_size = jax.random.fold_in(key, 23)
    keep = jax.random.randint(key_keep, (BRANCHES,), 0, 4) > 0
    sizes = 128 * jax.random.randint(key_size, (BRANCHES,), 1, BLEN // 128 + 1)
    lengths = jnp.where(keep, sizes, 0)
    return lengths.at[0].set(BLEN).astype(jnp.int32)


def with_ends(values, key, low, top_value):
    dims = values.shape
    spot = [jax.random.randint(jax.random.fold_in(key, axis), (), 0, dims[axis]) for axis in range(len(dims))]
    values = values.at[tuple(spot)].set(low)
    longest = dims.index(max(dims))
    spot[longest] = (spot[longest] + 1) % dims[longest]
    return values.at[tuple(spot)].set(top_value)


def steps_of(key, shape, split, smallest, largest):
    def one(dim, blocks):
        steps = jax.random.uniform(jax.random.fold_in(jax.random.fold_in(key, 6), dim), (blocks,), jnp.float32, smallest / len(split), largest / len(split))
        return jnp.repeat(jnp.exp(steps), shape[dim] // blocks).reshape((-1,) + (1,) * (len(shape) - dim - 1))

    factor_of = one(*split[0])
    for cut in split[1:]:
        factor_of = factor_of * one(*cut)
    return factor_of


def gaussian(rng, shape, deviation, most, split=(), kind=jnp.bfloat16):
    gain = steps_of(rng, shape, split, -0.22, 0.18) if split else 1.0
    values = jax.random.normal(rng, shape, jnp.float32) * deviation * gain
    return jnp.minimum(jnp.maximum(values, -most), most).astype(kind)


def setup_inputs(seed: int = 0) -> dict:
    seeds = jax.random.split(jax.random.key(seed), 10)
    trunk_tokens = gaussian(seeds[0], (TREES, TRUNK_LEN, D), 1.0, 6.0, ((0, 4), (1, 8)))
    branch_tokens = gaussian(seeds[1], (BRANCHES, BLEN, D), 1.0, 6.0, ((0, 32),))
    fork_offset = with_ends(jax.random.randint(seeds[2], (N_LEAF, N_TRUNK, SLOTS), 0, TRUNK_TOK), jax.random.fold_in(seeds[2], 1), 0, TRUNK_TOK - 1).astype(jnp.int32)
    fork_tree = with_ends(jax.random.randint(seeds[3], (N_LEAF, N_TRUNK, SLOTS), 0, TREES_DEV), jax.random.fold_in(seeds[3], 1), 0, TREES_DEV - 1).astype(jnp.int32)
    branch_len = draw_branch_len(jax.random.fold_in(seeds[9], 71), 0)
    w_query = gaussian(seeds[5], (D, HD), D ** -0.5, 0.1875, ((0, 8),))
    w_key = gaussian(seeds[6], (D, HD), D ** -0.5, 0.1875, ((0, 8),))
    w_value = gaussian(seeds[7], (D, HD), D ** -0.5, 0.1875, ((0, 8),))
    w_out = gaussian(seeds[8], (HD, D), HD ** -0.5, 0.1875, ((0, 8),))
    return dict(trunk_tokens=trunk_tokens, branch_tokens=branch_tokens, fork_offset=fork_offset, fork_tree=fork_tree, branch_len=branch_len, w_query=w_query, w_key=w_key, w_value=w_value, w_out=w_out)


def tree_states(tokens, w_key, w_value):
    keys = jnp.dot(tokens, w_key, preferred_element_type=jnp.float32).astype(jnp.bfloat16)
    values = jnp.dot(tokens, w_value, preferred_element_type=jnp.float32).astype(jnp.bfloat16)
    key_four = keys.reshape(N_TRUNK, TRUNK_TOK, H, DH).astype(jnp.float32)
    value_four = values.reshape(N_TRUNK, TRUNK_TOK, H, DH).astype(jnp.float32)
    totals = jnp.einsum('sthd,sthf->shdf', key_four, value_four)
    prefix = jnp.cumsum(totals, axis=0) - totals
    return (keys, values, prefix)

def branch_output(tokens, state, live_len, w_query, w_key, w_value, w_out):
    query = jnp.dot(tokens, w_query, preferred_element_type=jnp.float32).astype(jnp.bfloat16)
    key = jnp.dot(tokens, w_key, preferred_element_type=jnp.float32).astype(jnp.bfloat16)
    value = jnp.dot(tokens, w_value, preferred_element_type=jnp.float32).astype(jnp.bfloat16)
    query = query.reshape(BLEN, H, DH).astype(jnp.float32)
    key = key.reshape(BLEN, H, DH).astype(jnp.float32)
    value = value.reshape(BLEN, H, DH).astype(jnp.float32)
    inter = jnp.einsum('bhd,hdf->bhf', query, state, precision=lax.Precision.HIGHEST)
    scores = jnp.einsum('bhd,chd->hbc', query, key)
    rows = jnp.arange(BLEN)
    causal = rows[None, :] <= rows[:, None]
    weights = jnp.where(causal[None], scores, 0.0).astype(jnp.bfloat16)
    numerator = inter + jnp.einsum('hbc,chf->bhf', weights.astype(jnp.float32), value)
    meansq = lax.optimization_barrier(jnp.mean(numerator * numerator, axis=-1, keepdims=True))
    normed = (numerator * lax.rsqrt(meansq + 1e-06)).astype(jnp.bfloat16).reshape(BLEN, HD)
    result = jnp.dot(normed, w_out, preferred_element_type=jnp.float32)
    live = rows < live_len
    return jnp.where(live[:, None], result, 0.0).astype(jnp.bfloat16)

def reference(trunk_tokens, branch_tokens, fork_offset, fork_tree, branch_len, w_query, w_key, w_value, w_out):
    all_keys, all_values, prefix = lax.map(lambda tokens: tree_states(tokens, w_key, w_value), trunk_tokens)
    positions = jnp.arange(TRUNK_TOK)

    def one_branch(index):
        owner = index // (N_TRUNK * SLOTS)
        shard = index // SLOTS % N_TRUNK
        within = index % SLOTS
        source = within // CAP
        column = owner * CAP + within % CAP
        offset = fork_offset[source, shard, column]
        tree = source * TREES_DEV + fork_tree[source, shard, column]
        start = (shard * TRUNK_TOK).astype(jnp.int32)
        tree_keys = lax.dynamic_index_in_dim(all_keys, tree, 0, keepdims=False)
        tree_values = lax.dynamic_index_in_dim(all_values, tree, 0, keepdims=False)
        rows_key = lax.dynamic_slice_in_dim(tree_keys, start, TRUNK_TOK, 0).astype(jnp.float32)
        rows_value = lax.dynamic_slice_in_dim(tree_values, start, TRUNK_TOK, 0).astype(jnp.float32)
        keep = (positions < offset).astype(jnp.float32)
        rows_key = (rows_key * keep[:, None]).reshape(TRUNK_TOK, H, DH)
        partial_value = jnp.einsum('thd,thf->hdf', rows_key, rows_value.reshape(TRUNK_TOK, H, DH))
        carried = prefix[tree, shard]
        state = carried + partial_value
        return branch_output(branch_tokens[index], state, branch_len[index], w_query, w_key, w_value, w_out)
    return lax.map(one_branch, jnp.arange(BRANCHES, dtype=jnp.int32))
```

```python
import functools

import jax
import jax.numpy as jnp
from jax import lax
from jax.experimental import pallas as pl
from jax.experimental.pallas import tpu as pltpu
from jax.sharding import PartitionSpec as P

H = 8
DH = 128
F32 = jnp.float32
BF16 = jnp.bfloat16
VMEM_BYTES = 48 * 1024 * 1024


def swap(value, axis, bit):
    return lax.ppermute(value, axis, [(i, i ^ bit) for i in range(lax.axis_size(axis))])


def dot(left, right):
    return jnp.dot(left, right, preferred_element_type=F32)


def vmem(count):
    return [pl.BlockSpec(memory_space=pltpu.VMEM)] * count


def smem(count):
    return [pl.BlockSpec(memory_space=pltpu.SMEM)] * count


def params():
    return pltpu.CompilerParams(vmem_limit_bytes=VMEM_BYTES)


def halves_kernel(count, *refs):
    core = lax.axis_index("trunk") % 2
    mine, other, outs = refs[:count], refs[count : 2 * count], refs[2 * count :]
    for a, b, out in zip(mine, other, outs):
        rows, width = a.shape
        half = width // 2
        columns = pl.ds(pl.multiple_of(core * half, half), half)
        first, second = a[:, columns], b[:, columns]
        out[pl.ds(pl.multiple_of(core * rows, rows), rows), :] = first
        out[pl.ds(pl.multiple_of((1 - core) * rows, rows), rows), :] = second


def chip_halves(mine, other):
    rows, width = mine[0].shape
    shape = jax.ShapeDtypeStruct((2 * rows, width // 2), mine[0].dtype)
    return pl.pallas_call(
        functools.partial(halves_kernel, len(mine)),
        out_shape=[shape] * len(mine),
        in_specs=vmem(2 * len(mine)),
        out_specs=vmem(len(mine)),
        compiler_params=params(),
    )(*mine, *other)


def gather_chips(value, bits):
    held, offsets = value[None], [0]
    for bit in bits:
        other = swap(held, "trunk", bit)
        other_offsets = [o ^ bit for o in offsets]
        if bit == bits[-1]:
            return [(held, offsets), (other, other_offsets)]
        held = jnp.concatenate([held, other])
        offsets = offsets + other_offsets
    return [(held, offsets)]


def in_order(pieces):
    held = jnp.concatenate([p for p, _ in pieces])
    offsets = [o // 2 for _, part in pieces for o in part]
    place = [offsets.index(i) for i in range(len(offsets))]
    chip = lax.axis_index("trunk") // 2
    order = jnp.asarray(place, jnp.int32)[chip ^ jnp.arange(len(place), dtype=jnp.int32)]
    held = jnp.take(held, order, axis=0)
    return [(held.reshape(1, -1, held.shape[-1]), [0])]


def project(x_ref, pieces, refs, columns):
    chip = lax.axis_index("trunk") // 2
    total = None
    for offsets, ref in zip(pieces, refs):
        depth = ref.shape[1]
        for slot, offset in enumerate(offsets):
            if len(pieces) == 1 and len(offsets) == 1:
                left = x_ref[...]
            else:
                start = (chip ^ (offset // 2)) * depth
                left = x_ref[:, pl.ds(pl.multiple_of(start, depth), depth)]
            term = dot(left, ref[slot, :, columns])
            total = term if total is None else total + term
    return total


def trunk_kernel(key_offsets, value_offsets, heads, entries, *refs):
    nk, nv = len(key_offsets), len(value_offsets)
    off_ref, tree_ref, xm_ref, xo_ref = refs[:4]
    k_refs = refs[4 : 4 + nk]
    v_refs = refs[4 + nk : 4 + nk + nv]
    total_ref, fork_ref, x_ref, state_ref = refs[4 + nk + nv :]
    side, tree = pl.program_id(0), pl.program_id(1)
    trees = pl.num_programs(1)
    core = lax.axis_index("trunk") % 2

    @pl.when(side == 0)
    def _():
        x_ref[...] = xm_ref[0]

    @pl.when(side == 1)
    def _():
        x_ref[...] = xo_ref[0]

    tok = x_ref.shape[0]
    keys = project(x_ref, key_offsets, k_refs, slice(None))
    values = project(x_ref, value_offsets, v_refs, slice(None)).astype(BF16)
    keys_t = keys.T.astype(BF16)
    place = lax.broadcasted_iota(jnp.int32, (DH, tok), 1)
    limits = [
        jnp.where(tree_ref[side, e] == tree, off_ref[side, e], 0) for e in range(entries)
    ]
    for h in range(heads):
        key_h = keys_t[h * DH : (h + 1) * DH]
        rows = [key_h] + [jnp.where(place < limit, key_h, jnp.zeros_like(key_h)) for limit in limits]
        product = dot(jnp.concatenate(rows), values[:, h * DH : (h + 1) * DH])
        state_ref[side, tree, h] = product[:DH]
        for e in range(entries):
            part = product[(e + 1) * DH : (e + 2) * DH]

            @pl.when(tree == 0)
            def _():
                fork_ref[side, e, h] = part

            @pl.when(tree != 0)
            def _():
                fork_ref[side, e, h] += part

    @pl.when((side == 1) & (tree == trees - 1))
    def _():
        total_ref[...] = (state_ref[0] + state_ref[1]).astype(BF16)
        for e in range(entries):
            fork_ref[1 - core, e] += state_ref[core, tree_ref[1 - core, e]]


def trunk_states(offsets, trees_of, mine, other, keys, values):
    trees, tok, width = mine.shape
    entries = offsets.shape[1]
    cols = keys[0][0].shape[-1]
    heads = cols // DH
    whole = lambda a: pl.BlockSpec(a.shape, lambda i, g: (0,) * a.ndim)
    pieces = [p for p, _ in keys] + [p for p, _ in values]
    kernel = functools.partial(
        trunk_kernel, [o for _, o in keys], [o for _, o in values], heads, entries
    )
    return pl.pallas_call(
        kernel,
        grid=(2, trees),
        out_shape=[
            jax.ShapeDtypeStruct((trees, heads, DH, DH), BF16),
            jax.ShapeDtypeStruct((2, entries, heads, DH, DH), F32),
        ],
        in_specs=smem(2)
        + [
            pl.BlockSpec((1, tok, width), lambda i, g: (jnp.where(i == 0, g, trees - 1), 0, 0)),
            pl.BlockSpec((1, tok, width), lambda i, g: (jnp.where(i == 0, 0, g), 0, 0)),
        ]
        + [whole(p) for p in pieces],
        out_specs=[
            pl.BlockSpec((trees, heads, DH, DH), lambda i, g: (0, 0, 0, 0)),
            pl.BlockSpec((2, entries, heads, DH, DH), lambda i, g: (0, 0, 0, 0, 0)),
        ],
        scratch_shapes=[
            pltpu.VMEM((tok, width), BF16),
            pltpu.VMEM((2, trees, heads, DH, DH), F32),
        ],
        compiler_params=params(),
        name="trunk_states",
    )(offsets, trees_of, mine, other, *pieces)


def scan_up(total, bits):
    index = lax.axis_index("trunk")
    terms, held = [], total
    for bit in bits:
        other = swap(held, "trunk", bit)
        terms.append((other, (index & bit) != 0))
        if bit != bits[-1]:
            held = (held.astype(F32) + other.astype(F32)).astype(BF16)
    return terms


def scan_down(total, bits):
    index = lax.axis_index("trunk")
    terms, lower = [], None
    for bit in bits[::-1]:
        message = jnp.where((index & bit) == 0, total.astype(F32), 0.0)
        if lower is not None:
            message = message + lower
        other = swap(message.astype(BF16), "trunk", bit)
        terms.append((other, None))
        lower = other.astype(F32) if lower is None else lower + other.astype(F32)
    return terms


def fork_kernel(masks, lanes, cap, *refs):
    n = len(masks)
    tree_ref, fork_ref = refs[:2]
    terms, outs, carried_ref = refs[2 : 2 + n], refs[2 + n : -1], refs[-1]
    index, lane = lax.axis_index("trunk"), lax.axis_index("leaf")
    carried = None
    for mask, ref in zip(masks, terms):
        term = ref[...].astype(F32)
        if mask:
            term = jnp.where((index & mask) != 0, term, 0.0)
        carried = term if carried is None else carried + term
    carried_ref[...] = carried
    for apart in range(lanes):
        for side in range(2):
            for c in range(cap):
                entry = (lane ^ apart) * cap + c
                state = fork_ref[side, entry] + carried_ref[tree_ref[side, entry]]
                outs[apart][side, c] = state.astype(BF16)


def fork_states(trees_of, forks, terms, masks, lanes):
    _, entries, heads = forks.shape[:3]
    cap = entries // lanes
    shape = jax.ShapeDtypeStruct((2, cap, heads, DH, DH), BF16)
    return pl.pallas_call(
        functools.partial(fork_kernel, masks, lanes, cap),
        out_shape=[shape] * lanes,
        in_specs=smem(1) + vmem(1 + len(terms)),
        out_specs=vmem(lanes),
        scratch_shapes=[pltpu.VMEM(terms[0].shape, F32)],
        compiler_params=params(),
        name="fork_states",
    )(trees_of, forks, *terms)


def branch_kernel(query_offsets, groups, blen, *refs):
    nq = len(query_offsets)
    flat = [offsets for pair in groups for offsets in pair]
    xm_ref, xo_ref = refs[:2]
    q_refs = refs[2 : 2 + nq]
    rest = list(refs[2 + nq : -3])
    kv = []
    for offsets in flat:
        kv.append(rest[: len(offsets)])
        rest = rest[len(offsets) :]
    q_out, intra_out, x_ref = refs[-3:]
    side = pl.program_id(0)

    @pl.when(side == 0)
    def _():
        x_ref[...] = xm_ref[...]

    @pl.when(side == 1)
    def _():
        x_ref[...] = xo_ref[...]

    queries = project(x_ref, query_offsets, q_refs, slice(None)).astype(BF16)
    q_out[0] = queries
    causal = lax.broadcasted_iota(jnp.int32, (blen, blen), 1) <= lax.broadcasted_iota(
        jnp.int32, (blen, blen), 0
    )
    column = 0
    for group in range(len(groups)):
        keys = project(x_ref, flat[2 * group], kv[2 * group], slice(None)).astype(BF16)
        values = project(x_ref, flat[2 * group + 1], kv[2 * group + 1], slice(None)).astype(BF16)
        for h in range(keys.shape[1] // DH):
            at = slice(h * DH, (h + 1) * DH)
            out_at = slice(column, column + DH)
            for start in range(0, x_ref.shape[0], blen):
                rows = slice(start, start + blen)
                scores = lax.dot_general(
                    queries[rows, out_at],
                    keys[rows, at],
                    (((1,), (1,)), ((), ())),
                    preferred_element_type=F32,
                )
                weights = jnp.where(causal, scores, 0.0).astype(BF16)
                intra_out[0, rows, out_at] = dot(weights, values[rows, at])
            column += DH


def branch_parts(mine, other, queries, groups, blen):
    rows, width = mine.shape
    block = 2 * blen if rows % (2 * blen) == 0 else blen
    steps = rows // block
    cols = queries[0][0].shape[-1]
    pieces = [p for p, _ in queries] + [p for pair in groups for part in pair for p, _ in part]
    whole = lambda a: pl.BlockSpec(a.shape, lambda i, g: (0,) * a.ndim)
    kernel = functools.partial(
        branch_kernel,
        [o for _, o in queries],
        [[[o for _, o in part] for part in pair] for pair in groups],
        blen,
    )
    return pl.pallas_call(
        kernel,
        grid=(2, steps),
        out_shape=[
            jax.ShapeDtypeStruct((2, rows, cols), BF16),
            jax.ShapeDtypeStruct((2, rows, cols), F32),
        ],
        in_specs=[
            pl.BlockSpec((block, width), lambda i, g: (jnp.where(i == 0, g, steps - 1), 0)),
            pl.BlockSpec((block, width), lambda i, g: (jnp.where(i == 0, 0, g), 0)),
        ]
        + [whole(p) for p in pieces],
        out_specs=[pl.BlockSpec((1, block, cols), lambda i, g: (i, g, 0))] * 2,
        scratch_shapes=[pltpu.VMEM((block, width), BF16)],
        compiler_params=params(),
        name="branch_parts",
    )(mine, other, *pieces)


def norm_kernel(lanes, cap, groups, *refs):
    q_ref, intra_ref = refs[:2]
    state_refs = refs[2:-2]
    outs = refs[-2:]
    lane = lax.axis_index("leaf")
    blen = q_ref.shape[2]
    for apart in range(lanes):
        for side in range(2):
            for c in range(cap):
                slot = (lane ^ apart) * cap + c
                column = 0
                for group in range(groups):
                    ref = state_refs[group * lanes + apart]
                    for h in range(ref.shape[2]):
                        at = slice(column, column + DH)
                        total = intra_ref[side, slot, :, at] + dot(
                            q_ref[side, slot, :, at], ref[side, c, h]
                        )
                        meansq = jnp.mean(total * total, axis=-1, keepdims=True)
                        outs[side][slot, :, at] = (total * lax.rsqrt(meansq + 1e-06)).astype(BF16)
                        column += DH


def norm_parts(queries, intra, states, lanes):
    _, slots, blen, cols = queries.shape
    shape = jax.ShapeDtypeStruct((slots, blen, cols), BF16)
    flat = [s for group in states for s in group]
    return pl.pallas_call(
        functools.partial(norm_kernel, lanes, slots // lanes, len(states)),
        out_shape=[shape] * 2,
        in_specs=vmem(2 + len(flat)),
        out_specs=vmem(2),
        compiler_params=params(),
        name="norm_parts",
    )(queries, intra, *flat)


def out_kernel(len_ref, mine_ref, other_ref, w_ref, out_ref):
    core = lax.axis_index("trunk") % 2
    slots, blen, half = mine_ref.shape
    first = w_ref[pl.ds(pl.multiple_of(core * half, half), half), :]
    second = w_ref[pl.ds(pl.multiple_of((1 - core) * half, half), half), :]
    row = lax.broadcasted_iota(jnp.int32, (blen, w_ref.shape[1]), 0)
    for slot in range(slots):
        total = dot(mine_ref[slot], first) + dot(other_ref[slot], second)
        out_ref[slot] = jnp.where(row < len_ref[slot], total, 0.0).astype(BF16)


def out_project(lengths, mine, other, weights):
    slots, blen, _ = mine.shape
    return pl.pallas_call(
        out_kernel,
        out_shape=jax.ShapeDtypeStruct((slots, blen, weights.shape[1]), BF16),
        in_specs=smem(1) + vmem(3),
        out_specs=pl.BlockSpec(memory_space=pltpu.VMEM),
        compiler_params=params(),
        name="out_project",
    )(lengths, mine, other, weights)


def shards(
    trunk_tokens, branch_tokens, fork_offset, fork_tree, branch_len, w_query, w_key, w_value, w_out
):
    trees, trunk_tok, width = trunk_tokens.shape
    slots, blen, _ = branch_tokens.shape
    lanes, count = lax.axis_size("leaf"), lax.axis_size("trunk")
    entries = fork_offset.shape[2]
    bits = [1 << i for i in range(1, count.bit_length() - 1)]
    index = lax.axis_index("trunk")
    natural = (2 * w_key.shape[0]) % DH != 0

    def arranged(pieces):
        return in_order(pieces) if natural else pieces

    key_other, value_other = swap(w_key, "trunk", 1), swap(w_value, "trunk", 1)
    key_half, value_half = chip_halves([w_key, w_value], [key_other, value_other])
    keys = arranged(gather_chips(key_half, bits))
    values = arranged(gather_chips(value_half, bits[::-1]))

    forks = jnp.stack([fork_offset.reshape(entries), fork_tree.reshape(entries)])
    forks_other = swap(forks, "trunk", 1)
    offsets = jnp.stack([forks[0], forks_other[0]])
    trees_of = jnp.stack([forks[1], forks_other[1]])
    trunk_other = swap(trunk_tokens, "trunk", 1)
    branch_other = swap(branch_tokens, "trunk", 1)

    totals, fork_parts = trunk_states(offsets, trees_of, trunk_tokens, trunk_other, keys, values)
    terms = scan_up(totals, bits)
    sends = fork_states(
        trees_of, fork_parts, [t for t, _ in terms], bits, lanes
    )
    received = [sends[0]] + [swap(sends[a], "leaf", a) for a in range(1, lanes)]

    query_other = swap(w_query, "trunk", 1)
    (query_half,) = chip_halves([w_query], [query_other])
    queries = arranged(gather_chips(query_half, bits[::-1]))
    out_pieces = gather_chips(w_out, bits)
    out_mine = jnp.concatenate([p for p, _ in out_pieces])
    out_offsets = [o for _, part in out_pieces for o in part]
    out_other = swap(out_mine, "trunk", 1)
    held = jnp.concatenate([out_mine, out_other])
    out_offsets = out_offsets + [o ^ 1 for o in out_offsets]
    place = jnp.asarray([out_offsets.index(i) for i in range(count)], jnp.int32)
    out_full = jnp.take(held, place[index ^ jnp.arange(count, dtype=jnp.int32)], axis=0)
    out_full = out_full.reshape(-1, w_out.shape[1])

    q, intra = branch_parts(
        branch_tokens.reshape(slots * blen, width),
        branch_other.reshape(slots * blen, width),
        queries,
        [(keys, values)],
        blen,
    )
    q = q.reshape(2, slots, blen, -1)
    intra = intra.reshape(2, slots, blen, -1)
    normed_mine, normed_other = norm_parts(q, intra, [received], lanes)
    normed_swapped = swap(normed_other, "trunk", 1)
    return out_project(branch_len, normed_mine, normed_swapped, out_full)


def solution(mesh):
    in_specs = (
        P("leaf", "trunk", None),
        P(("leaf", "trunk"), None, None),
        P("leaf", "trunk", None),
        P("leaf", "trunk", None),
        P(("leaf", "trunk")),
        P("trunk", None),
        P("trunk", None),
        P("trunk", None),
        P("trunk", None),
    )
    out_specs = P(("leaf", "trunk"), None, None)
    return jax.shard_map(shards, mesh=mesh, in_specs=in_specs, out_specs=out_specs, check_vma=False)
```

```python
import functools

import jax
import jax.numpy as jnp
from jax import lax
from jax.experimental import pallas as pl
from jax.experimental.pallas import tpu as pltpu
from jax.sharding import PartitionSpec as P

H = 8
DH = 128
F32 = jnp.float32
BF16 = jnp.bfloat16
VMEM_BYTES = 16 * 1024 * 1024
ANY = pl.BlockSpec(memory_space=pl.ANY)
VMEM = pl.BlockSpec(memory_space=pltpu.VMEM)
SMEM = pl.BlockSpec(memory_space=pltpu.SMEM)


def swap(value, axis, bit, name="rows"):
    with jax.named_scope("to_" + name):
        return lax.ppermute(value, axis, [(i, i ^ bit) for i in range(lax.axis_size(axis))])


def dot(left, right):
    return jnp.dot(left, right, preferred_element_type=F32)


def shape_of(shape, dtype=BF16):
    return jax.ShapeDtypeStruct(tuple(shape), dtype)


def call(kernel, name, outs, inputs, specs, out_specs=None, scratch=(), order=None, through=(), landed=(), weight=0.0):
    after = (*(order or ()), *landed)
    n, t, w, m = len(inputs), len(through), len(after), len(outs)

    def body(*refs):
        kernel(*refs[:n], *refs[n + t + w : n + t + w + m], *refs[n + 2 * t + w + m :])

    results = pl.pallas_call(
        body,
        out_shape=[*outs, *(shape_of(a.shape, a.dtype) for a in through)],
        in_specs=[*specs, *[ANY] * (t + w)],
        out_specs=[*(out_specs or [VMEM] * m), *[ANY] * t],
        scratch_shapes=list(scratch),
        input_output_aliases={n + i: m + i for i in range(t)},
        compiler_params=pltpu.CompilerParams(vmem_limit_bytes=VMEM_BYTES),
        cost_estimate=pl.CostEstimate(
            flops=int(weight * 1e9), bytes_accessed=0, transcendentals=0
        ),
        name=name,
    )(*inputs, *through, *after)
    if order is not None:
        order[:] = [results[0]]
    return results


def core_index():
    return lax.axis_index("trunk") % 2


def chip_index():
    return lax.axis_index("trunk") // 2


def touch_kernel(*refs):
    refs[-1][...] = jnp.zeros_like(refs[-1])


def touch(arrays, **rest):
    return call(touch_kernel, "touch", [shape_of((8, DH), F32)], arrays, [ANY] * len(arrays), **rest)


def halves_kernel(count, chosen, *refs):
    core = core_index()
    mine, other, outs, sem = refs[:count], refs[count : 2 * count], refs[2 * count : -1], refs[-1]
    copies = []
    for out, (parts, picks) in zip(outs, chosen):
        for slot, (i, p, own) in enumerate(picks):
            rows, width = mine[i].shape
            part = width // 2 // parts
            first = (core if own else 1 - core) * (width // 2) + p * part
            columns = pl.ds(pl.multiple_of(first, part), part)
            for source, place in ((mine[i], core), (other[i], 1 - core)):
                target = out.at[slot, pl.ds(pl.multiple_of(place * rows, rows), rows)]
                copies.append(
                    pltpu.make_async_copy(source.at[:, columns], target, sem.at[len(copies)])
                )
    for copy in copies:
        copy.start()
    for copy in copies:
        copy.wait()


def chip_halves(mine, other, chosen, **rest):
    rows, width = mine[0].shape
    return call(
        functools.partial(halves_kernel, len(mine), chosen),
        "chip_halves",
        [shape_of((len(picks), 2 * rows, width // 2 // parts)) for parts, picks in chosen],
        [*mine, *other],
        [ANY] * (2 * len(mine)),
        scratch=[pltpu.SemaphoreType.DMA((sum(2 * len(picks) for _, picks in chosen),))],
        **rest,
    )


def ahead_kernel(first_ref, second_ref, first_out, second_out, sem):
    copies = [
        pltpu.make_async_copy(first_ref.at[0], first_out, sem.at[0]),
        pltpu.make_async_copy(second_ref.at[1], second_out, sem.at[1]),
    ]
    for copy in copies:
        copy.start()
    for copy in copies:
        copy.wait()


def send_pair(pair, bits, name):
    return [pair, *(swap(pair, "trunk", bit, name) for bit in bits)]


def send_direct(pair, bits, name):
    steps = [0, bits[0], bits[1], bits[0] ^ bits[1]]
    arrays = [pair, *(swap(pair, "trunk", step, name) for step in steps[1:])]
    return arrays, [[(i, (slot,), steps[i] // 2) for i in range(4)] for slot in range(2)]


def send_ahead(held, bits, name, through=(), **rest):
    first, second = bits
    _, rows, cols = held[0].shape
    out = call(
        ahead_kernel,
        "send_ahead",
        [shape_of((rows, cols))] * 2,
        held[1:],
        [ANY] * 2,
        scratch=[pltpu.SemaphoreType.DMA((2,))],
        through=through,
        **rest,
    )
    far = [
        swap(out[0], "trunk", second, name + "_ahead"),
        swap(out[1], "trunk", first, name + "_ahead"),
    ]
    steps = (0, first // 2, second // 2, (first ^ second) // 2)
    picks = [
        [(i, (slot,), steps[i]) for i in range(3)] + [(3 + slot, (), steps[3])] for slot in range(2)
    ]
    return ([*held, *far], picks), out[2:]


def whole_pair(weights, parts, chosen):
    arrays = []
    for i, p in chosen:
        full = lax.all_gather(weights[i], "trunk", axis=0, tiled=True)
        part = full.shape[1] // 2 // parts
        start = core_index() * (full.shape[1] // 2) + p * part
        arrays.append(lax.dynamic_slice_in_dim(full, start, part, axis=1))
    return arrays, [[(i, (), None)] for i in range(len(arrays))]


def project(x_ref, lead, picks, refs):
    chip = chip_index()
    total = None
    for number, index, offset in picks:
        weight = refs[number][index] if index else refs[number][...]
        depth = weight.shape[0]
        if offset is None:
            left = x_ref[lead]
        else:
            left = x_ref[lead, :, pl.ds(pl.multiple_of((chip ^ offset) * depth, depth), depth)]
        term = dot(left, weight)
        total = term if total is None else total + term
    return total


def pack_kernel(offset_ref, tree_ref, out_ref):
    out_ref[0:1] = offset_ref[0]
    out_ref[1:2] = tree_ref[0]


def pack_forks(offset, tree, **rest):
    return call(
        pack_kernel,
        "pack_forks",
        [shape_of((2, offset.shape[2]), jnp.int32)],
        [offset, tree],
        [VMEM] * 2,
        **rest,
    )[0]


def trunk_kernel(picks, mask, *refs):
    xs, weights = refs[:2], refs[2:-6]
    low_ref, high_ref, first_ref, keys_ref, values_ref, state_ref = refs[-6:]
    top = (lax.axis_index("trunk") & mask) == 0
    trees, heads = state_ref.shape[1:3]
    low = low_ref.shape[1]
    for side in range(2):
        for tree in range(trees):
            keys = project(xs[side], tree, picks[0], weights).astype(BF16)
            values = project(xs[side], tree, picks[1], weights).astype(BF16)
            keys_ref[side, tree] = keys
            values_ref[side, tree] = values
            for h in range(heads):
                at = slice(h * DH, (h + 1) * DH)
                state = lax.dot_general(
                    keys[:, at], values[:, at], (((0,), (0,)), ((), ())), preferred_element_type=F32
                )
                state_ref[side, tree, h] = state
                if side:
                    total = (state_ref[0, tree, h] + state).astype(BF16)
                    if h < low:
                        low_ref[tree, h] = total
                    else:
                        high_ref[tree, h - low] = total
                        first_ref[tree, h - low] = jnp.where(top, total, jnp.zeros_like(total))


def trunk_states(mine, other, weights, mask, **rest):
    trees, tok, width = mine.shape
    arrays, picks = weights
    cols = arrays[0].shape[-1]
    heads = cols // DH
    low = heads // 2
    return call(
        functools.partial(trunk_kernel, picks, mask),
        "trunk_states",
        [
            shape_of((trees, low, DH, DH)),
            shape_of((trees, heads - low, DH, DH)),
            shape_of((trees, heads - low, DH, DH)),
            shape_of((2, trees, tok, cols)),
            shape_of((2, trees, tok, cols)),
            shape_of((2, trees, heads, DH, DH), F32),
        ],
        [mine, other, *arrays],
        [VMEM] * (2 + len(arrays)),
        **rest,
    )


def part_kernel(mine_ref, other_ref, keys_ref, values_ref, state_ref, fork_ref):
    core = core_index()
    tok = keys_ref.shape[2]
    entries, heads = fork_ref.shape[1:3]
    place = lax.broadcasted_iota(jnp.int32, (tok, DH), 0)
    for side in range(2):
        ints = other_ref if side else mine_ref
        for e in range(entries):
            tree = ints[1, e]
            inside = place < ints[0, e]
            odd = core != side
            for h in range(heads):
                at = slice(h * DH, (h + 1) * DH)
                keys = keys_ref[side, tree, :, at]
                part = lax.dot_general(
                    jnp.where(inside, keys, jnp.zeros_like(keys)),
                    values_ref[side, tree, :, at],
                    (((0,), (0,)), ((), ())),
                    preferred_element_type=F32,
                )
                lower = state_ref[1 - side, tree, h]
                fork_ref[side, e, h] = part + jnp.where(odd, lower, jnp.zeros_like(lower))


def fork_parts(forks, keys, values, states, **rest):
    _, _, tok, cols = keys.shape
    entries, heads = forks[0].shape[1], cols // DH
    return call(
        part_kernel,
        "fork_parts",
        [shape_of((2, entries, heads, DH, DH), F32)],
        [*forks, keys, values, states],
        [SMEM] * 2 + [VMEM] * 3,
        **rest,
    )


def scan_kernel(mask, low_ref, low_in_ref, high_ref, *refs):
    high_in, (low_out, high_out) = refs[:-2], refs[-2:]
    low_out[...] = (low_ref[...].astype(F32) + low_in_ref[...].astype(F32)).astype(BF16)
    total = jnp.where((lax.axis_index("trunk") & mask) == 0, high_ref[...].astype(F32), 0.0)
    for ref in high_in:
        total = total + ref[...].astype(F32)
    high_out[...] = total.astype(BF16)


def scan_step(low, low_in, high, high_in, mask, **rest):
    return call(
        functools.partial(scan_kernel, mask),
        "scan_step",
        [shape_of(low.shape), shape_of(high.shape)],
        [low, low_in, high, *high_in],
        [VMEM] * (3 + len(high_in)),
        **rest,
    )


def fork_kernel(low_masks, high_masks, lanes, *refs):
    ints, fork_ref, terms = refs[:2], refs[2], refs[3:]
    low_refs = terms[: len(low_masks)]
    high_refs = terms[len(low_masks) : len(low_masks) + len(high_masks)]
    outs, carried_ref = refs[-1 - lanes : -1], refs[-1]
    index, lane = lax.axis_index("trunk"), lax.axis_index("leaf")
    cap = outs[0].shape[1]
    first = 0
    for masks, terms in ((low_masks, low_refs), (high_masks, high_refs)):
        carried = None
        for mask, ref in zip(masks, terms):
            term = ref[...].astype(F32)
            if mask:
                term = jnp.where((index & mask) != 0, term, jnp.zeros_like(term))
            carried = term if carried is None else carried + term
        if terms:
            heads = terms[0].shape[1]
            carried_ref[:, first : first + heads] = carried
            first += heads
    for apart in range(lanes):
        for side in range(2):
            for c in range(cap):
                entry = (lane ^ apart) * cap + c
                state = fork_ref[side, entry] + carried_ref[ints[side][1, entry]]
                outs[apart][side, c] = state.astype(BF16)


def fork_states(forks, parts, low, high, lanes, **rest):
    _, entries, heads = parts.shape[:3]
    terms = [t for t, _ in low] + high
    trees = terms[0].shape[0]
    return call(
        functools.partial(fork_kernel, [m for _, m in low], [0] * len(high), lanes),
        "fork_states",
        [shape_of((2, entries // lanes, heads, DH, DH))] * lanes,
        [*forks, parts, *terms],
        [SMEM] * 2 + [VMEM] * (1 + len(terms)),
        scratch=[pltpu.VMEM((trees, heads, DH, DH), F32)],
        **rest,
    )


def branch_kernel(query_picks, picks, count, blen, *refs):
    xs, query_refs, weights = refs[:2], refs[2 : 2 + count], refs[2 + count : -2]
    q_out, intra_out = refs[-2:]
    rows = xs[0].shape[1]
    row = lax.broadcasted_iota(jnp.int32, (rows, rows), 0)
    column = lax.broadcasted_iota(jnp.int32, (rows, rows), 1)
    seen = (column <= row) & (column >= row - lax.rem(row, blen))
    for side in range(2):
        for slot in range(xs[0].shape[0]):
            first = 0
            for part in query_picks:
                q = project(xs[side], slot, part, query_refs).astype(BF16)
                q_out[side, slot, :, first : first + q.shape[1]] = q
                first += q.shape[1]
            k = project(xs[side], slot, picks[0], weights).astype(BF16)
            v = project(xs[side], slot, picks[1], weights).astype(BF16)
            for h in range(k.shape[1] // DH):
                at = slice(h * DH, (h + 1) * DH)
                scores = lax.dot_general(
                    q_out[side, slot, :, at],
                    k[:, at],
                    (((1,), (1,)), ((), ())),
                    preferred_element_type=F32,
                )
                scores = jnp.where(seen, scores, 0.0).astype(BF16)
                intra_out[side, slot, :, at] = dot(scores, v[:, at])


def branch_parts(mine, other, queries, weights, **rest):
    slots, blen, width = mine.shape
    join = 2 if slots % 2 == 0 else 1
    mine, other = (a.reshape(slots // join, join * blen, width) for a in (mine, other))
    arrays = [*queries[0], *weights[0]]
    cols = weights[0][0].shape[-1]
    lead = (2, slots // join, join * blen, cols)
    outs = call(
        functools.partial(branch_kernel, queries[1], weights[1], len(queries[0]), blen),
        "branch_parts",
        [shape_of(lead), shape_of(lead, F32)],
        [mine, other, *arrays],
        [VMEM] * (2 + len(arrays)),
        **rest,
    )
    return [o.reshape(2, slots, blen, cols) for o in outs]


def norm_kernel(lanes, q_ref, intra_ref, *refs):
    states, outs = refs[:lanes], refs[lanes:]
    lane = lax.axis_index("leaf")
    cap, heads = states[0].shape[1:3]
    for apart in range(lanes):
        for side in range(2):
            for c in range(cap):
                slot = (lane ^ apart) * cap + c
                for h in range(heads):
                    at = slice(h * DH, (h + 1) * DH)
                    total = intra_ref[side, slot, :, at] + dot(
                        q_ref[side, slot, :, at], states[apart][side, c, h]
                    )
                    meansq = jnp.mean(total * total, axis=-1, keepdims=True)
                    normed = (total * lax.rsqrt(meansq + 1e-06)).astype(BF16)
                    if side == 0:
                        outs[0][slot, :, at] = normed
                    elif h < heads // 2:
                        outs[1][slot, :, at] = normed
                    else:
                        outs[2][slot, :, (h - heads // 2) * DH : (h - heads // 2 + 1) * DH] = normed


def norm_parts(queries, intra, states, **rest):
    _, slots, blen, cols = queries.shape
    return call(
        functools.partial(norm_kernel, len(states)),
        "norm_parts",
        [shape_of((slots, blen, w)) for w in (cols, cols // 2, cols // 2)],
        [queries, intra, *states],
        [VMEM] * (2 + len(states)),
        **rest,
    )


def place_kernel(picks, *refs):
    core, chip = core_index(), chip_index()
    sources, out_ref, sem = refs[:-2], refs[-2], refs[-1]
    copies = []
    for slot, number, index, offset in picks:
        source = sources[number].at[index] if index else sources[number]
        rows, half = source.shape
        first = (core if slot == 0 else 1 - core) * half
        target = out_ref.at[
            pl.ds(pl.multiple_of((chip ^ offset) * rows, rows), rows),
            pl.ds(pl.multiple_of(first, half), half),
        ]
        copies.append(pltpu.make_async_copy(source, target, sem.at[len(copies)]))
    for copy in copies:
        copy.start()
    for copy in copies:
        copy.wait()


def place_rows(weights, shape, **rest):
    arrays, picks = weights
    chosen = [(slot, *pick) for slot, part in enumerate(picks) for pick in part]
    return call(
        functools.partial(place_kernel, chosen),
        "place_rows",
        [shape_of(shape)],
        arrays,
        [ANY] * len(arrays),
        scratch=[pltpu.SemaphoreType.DMA((len(chosen),))],
        **rest,
    )[0]


def rows_of(w_ref, first, core, count):
    half = w_ref.shape[0] // 2
    return w_ref[pl.ds(pl.multiple_of(core * half + first, count), count), :]


def out_sum_kernel(first, terms, *refs):
    inputs, w_ref, out_ref = refs[: len(terms)], refs[len(terms)], refs[-1]
    core = core_index()
    slots, _, cols = inputs[0].shape
    weights = [rows_of(w_ref, f, core if own else 1 - core, cols) for f, own in terms]
    for slot in range(slots):
        total = refs[len(terms) + 1][slot] if first else None
        for ref, weight in zip(inputs, weights):
            term = dot(ref[slot], weight)
            total = term if total is None else total + term
        out_ref[slot] = total


def out_sum(inputs, terms, weights, total=None, **rest):
    slots, blen, cols = inputs[0].shape
    extra = [] if total is None else [total]
    return call(
        functools.partial(out_sum_kernel, total is not None, terms),
        "out_sum",
        [shape_of((slots, blen, weights.shape[1]), F32)],
        [*inputs, weights, *extra],
        [VMEM] * (len(inputs) + 1 + len(extra)),
        **rest,
    )[0]


def out_last_kernel(count, len_ref, *refs):
    inputs, (w_ref, total_ref, out_ref, held_ref, sem) = refs[:count], refs[count:]
    core = core_index()
    slots, blen, cols = inputs[0].shape
    weights = [rows_of(w_ref, i * cols, 1 - core, cols) for i in range(count)]
    row = lax.broadcasted_iota(jnp.int32, (blen, w_ref.shape[1]), 0)
    copies = []
    for slot in range(slots):
        total = total_ref[slot]
        for ref, weight in zip(inputs, weights):
            total = total + dot(ref[slot], weight)
        held_ref[slot] = jnp.where(row < len_ref[slot], total, 0.0).astype(BF16)
        copies.append(pltpu.make_async_copy(held_ref.at[slot], out_ref.at[slot], sem.at[slot]))
        copies[-1].start()
    for copy in copies:
        copy.wait()


def out_last(lengths, inputs, weights, total, **rest):
    slots, blen, _ = inputs[0].shape
    shape = (slots, blen, weights.shape[1])
    return call(
        functools.partial(out_last_kernel, len(inputs)),
        "out_last",
        [shape_of(shape)],
        [lengths, *inputs, weights, total],
        [SMEM] + [VMEM] * (2 + len(inputs)),
        [ANY],
        scratch=[pltpu.VMEM(shape, BF16), pltpu.SemaphoreType.DMA((slots,))],
        **rest,
    )[0]


def shards(
    trunk_tokens, branch_tokens, fork_offset, fork_tree, branch_len, w_query, w_key, w_value, w_out
):
    lanes, count = lax.axis_size("leaf"), lax.axis_size("trunk")
    bits = [1 << i for i in range(1, count.bit_length() - 1)]
    paired = len(bits) == 2 and (2 * w_key.shape[0]) % DH == 0
    order = []

    if paired:
        kv, qo = [w_key, w_value], [w_query, w_out]
        kv_other = [swap(w, "trunk", 1, "core") for w in kv]
        touch(kv, order=order)
        (pair,) = chip_halves(kv, kv_other, [(1, [(0, 0, True), (1, 0, True)])], order=order)
        held = send_pair(pair, bits, "kv")
        qo_other = [swap(w, "trunk", 1, "core") for w in qo]
    own_forks = pack_forks(fork_offset, fork_tree, order=order)
    forks = (own_forks, swap(own_forks, "trunk", 1, "forks"))
    trunk_other = swap(trunk_tokens, "trunk", 1, "tokens")
    branch_other = swap(branch_tokens, "trunk", 1, "tokens")
    if paired:
        chosen = [(2, [(0, 0, True), (0, 1, True)]), (1, [(1, 0, True), (1, 0, False)])]
        query_pair, out_pair = chip_halves(qo, qo_other, chosen, order=order)
        pair, _ = send_ahead(held, bits, "kv", order=order)
        ready = [*pair[0][3:], branch_other, forks[1]]
        _, query_pair = touch(ready, order=order, through=[query_pair])
        queries = send_direct(query_pair, bits, "query")
    else:
        pair = whole_pair([w_key, w_value], 1, [(0, 0), (1, 0)])
        queries = whole_pair([w_query], 2, [(0, 0), (0, 1)])
        out_full = lax.all_gather(w_out, "trunk", axis=0, tiled=True)

    low, high, message, *kept = trunk_states(trunk_tokens, trunk_other, pair, bits[-1], order=order)
    low_terms, high_terms = [], []
    for step, (up, down) in enumerate(zip(bits, bits[::-1])):
        if step:
            low, message = scan_step(low, low_terms[-1][0], high, high_terms, down, order=order)
        low_terms.append((swap(low, "trunk", up, "scan"), up))
        high_terms.append(swap(message, "trunk", down, "scan"))
        if not step:
            (parts,) = fork_parts(forks, *kept, order=order)
    passed = []
    if paired:
        touch(queries[0][1:], order=order, weight=10.0)
        passed = [out_pair]
    sends = fork_states(
        forks, parts, low_terms, high_terms, lanes, order=order, through=passed
    )
    far = sorted(range(1, lanes), key=lambda a: a == 1)
    moved = {a: swap(sends[a], "leaf", a, "lane") for a in far}
    received = [sends[0]] + [moved[a] for a in range(1, lanes)]
    if paired:
        held = send_pair(sends[lanes], bits, "out")
    q, intra = branch_parts(branch_tokens, branch_other, queries, pair, order=order)
    if paired:
        outs, _ = send_ahead(held, bits, "out", order=order)
    mine, *other = norm_parts(q, intra, received, order=order)
    other = [swap(o, "trunk", 1, "normed") for o in other]
    if paired:
        out_full = place_rows(outs, (w_out.shape[0] * count, w_out.shape[1]), order=order)
    total = out_sum([mine], [(0, True)], out_full, order=order, weight=4.0)
    return out_last(branch_len, other, out_full, total, order=order)


def solution(mesh):
    in_specs = (
        P("leaf", "trunk", None),
        P(("leaf", "trunk"), None, None),
        P("leaf", "trunk", None),
        P("leaf", "trunk", None),
        P(("leaf", "trunk")),
        P("trunk", None),
        P("trunk", None),
        P("trunk", None),
        P("trunk", None),
    )
    out_specs = P(("leaf", "trunk"), None, None)
    return jax.shard_map(shards, mesh=mesh, in_specs=in_specs, out_specs=out_specs, check_vma=False)
```

```python
import functools

import jax
import jax.numpy as jnp
from jax import lax
from jax.experimental import pallas as pl
from jax.experimental.pallas import tpu as pltpu
from jax.sharding import PartitionSpec as P

H = 8
DH = 128
F32 = jnp.float32
BF16 = jnp.bfloat16
VMEM_BYTES = 16 * 1024 * 1024
ANY = pl.BlockSpec(memory_space=pl.ANY)
VMEM = pl.BlockSpec(memory_space=pltpu.VMEM)
SMEM = pl.BlockSpec(memory_space=pltpu.SMEM)


def swap(value, axis, bit, name="rows"):
    with jax.named_scope("to_" + name):
        return lax.ppermute(value, axis, [(i, i ^ bit) for i in range(lax.axis_size(axis))])


def dot(left, right):
    return jnp.dot(left, right, preferred_element_type=F32)


def shape_of(shape, dtype=BF16):
    return jax.ShapeDtypeStruct(tuple(shape), dtype)


def call(kernel, name, outs, inputs, specs, out_specs=None, scratch=(), order=None, through=(), landed=(), weight=0.0):
    after = (*(order or ()), *landed)
    n, t, w, m = len(inputs), len(through), len(after), len(outs)

    def body(*refs):
        kernel(*refs[:n], *refs[n + t + w : n + t + w + m], *refs[n + 2 * t + w + m :])

    results = pl.pallas_call(
        body,
        out_shape=[*outs, *(shape_of(a.shape, a.dtype) for a in through)],
        in_specs=[*specs, *[ANY] * (t + w)],
        out_specs=[*(out_specs or [VMEM] * m), *[ANY] * t],
        scratch_shapes=list(scratch),
        input_output_aliases={n + i: m + i for i in range(t)},
        compiler_params=pltpu.CompilerParams(vmem_limit_bytes=VMEM_BYTES),
        cost_estimate=pl.CostEstimate(
            flops=int(weight * 1e9), bytes_accessed=0, transcendentals=0
        ),
        name=name,
    )(*inputs, *through, *after)
    if order is not None:
        order[:] = [results[0]]
    return results


def core_index():
    return lax.axis_index("trunk") % 2


def chip_index():
    return lax.axis_index("trunk") // 2


def touch_kernel(*refs):
    refs[-1][...] = jnp.zeros_like(refs[-1])


def touch(arrays, **rest):
    return call(touch_kernel, "touch", [shape_of((8, DH), F32)], arrays, [ANY] * len(arrays), **rest)


def halves_kernel(count, chosen, *refs):
    core, odd = core_index(), lax.axis_index("leaf") % 2
    mine, other, outs, sem = refs[:count], refs[count : 2 * count], refs[2 * count : -1], refs[-1]
    copies = []
    for out, (parts, picks) in zip(outs, chosen):
        for slot, (i, p, own) in enumerate(picks):
            rows, width = mine[i].shape
            part = width // 2 // parts
            p = {"even": odd, "odd": 1 - odd}.get(p, p)
            first = (core if own else 1 - core) * (width // 2) + p * part
            columns = pl.ds(pl.multiple_of(first, part), part)
            for source, place in ((mine[i], core), (other[i], 1 - core)):
                target = out.at[slot, pl.ds(pl.multiple_of(place * rows, rows), rows)]
                copies.append(
                    pltpu.make_async_copy(source.at[:, columns], target, sem.at[len(copies)])
                )
    for copy in copies:
        copy.start()
    for copy in copies:
        copy.wait()


def chip_halves(mine, other, chosen, **rest):
    rows, width = mine[0].shape
    return call(
        functools.partial(halves_kernel, len(mine), chosen),
        "chip_halves",
        [shape_of((len(picks), 2 * rows, width // 2 // parts)) for parts, picks in chosen],
        [*mine, *other],
        [ANY] * (2 * len(mine)),
        scratch=[pltpu.SemaphoreType.DMA((sum(2 * len(picks) for _, picks in chosen),))],
        **rest,
    )


def ahead_kernel(first_ref, second_ref, first_out, second_out, sem):
    copies = [
        pltpu.make_async_copy(first_ref.at[0], first_out, sem.at[0]),
        pltpu.make_async_copy(second_ref.at[1], second_out, sem.at[1]),
    ]
    for copy in copies:
        copy.start()
    for copy in copies:
        copy.wait()


def send_pair(pair, bits, name):
    return [pair, *(swap(pair, "trunk", bit, name) for bit in bits)]


def send_across(part, other, bits, name):
    steps = [0, bits[0], bits[1], bits[0] ^ bits[1]]
    near = [swap(part, "trunk", step, name) for step in steps[1:]]
    across = [swap(a, "leaf", 1, name + "_lane") for a in near]
    arrays = [part, *near, other, *across]
    return arrays, [[(4 * i + k, (0,), steps[k] // 2) for k in range(4)] for i in range(2)]


def send_ahead(held, bits, name, through=(), **rest):
    first, second = bits
    _, rows, cols = held[0].shape
    out = call(
        ahead_kernel,
        "send_ahead",
        [shape_of((rows, cols))] * 2,
        held[1:],
        [ANY] * 2,
        scratch=[pltpu.SemaphoreType.DMA((2,))],
        through=through,
        **rest,
    )
    far = [
        swap(out[0], "trunk", second, name + "_ahead"),
        swap(out[1], "trunk", first, name + "_ahead"),
    ]
    steps = (0, first // 2, second // 2, (first ^ second) // 2)
    picks = [
        [(i, (slot,), steps[i]) for i in range(3)] + [(3 + slot, (), steps[3])] for slot in range(2)
    ]
    return ([*held, *far], picks), out[2:]


def whole_pair(weights, parts, chosen):
    arrays = []
    for i, p in chosen:
        full = lax.all_gather(weights[i], "trunk", axis=0, tiled=True)
        part = full.shape[1] // 2 // parts
        start = core_index() * (full.shape[1] // 2) + p * part
        arrays.append(lax.dynamic_slice_in_dim(full, start, part, axis=1))
    return arrays, [[(i, (), None)] for i in range(len(arrays))]


def project(x_ref, lead, picks, refs):
    chip = chip_index()
    total = None
    for number, index, offset in picks:
        weight = refs[number][index] if index else refs[number][...]
        depth = weight.shape[0]
        if offset is None:
            left = x_ref[lead]
        else:
            left = x_ref[lead, :, pl.ds(pl.multiple_of((chip ^ offset) * depth, depth), depth)]
        term = dot(left, weight)
        total = term if total is None else total + term
    return total


def pack_kernel(offset_ref, tree_ref, out_ref):
    out_ref[0:1] = offset_ref[0]
    out_ref[1:2] = tree_ref[0]


def pack_forks(offset, tree, **rest):
    return call(
        pack_kernel,
        "pack_forks",
        [shape_of((2, offset.shape[2]), jnp.int32)],
        [offset, tree],
        [VMEM] * 2,
        **rest,
    )[0]


def partial_kernel(picks, *refs):
    xs, weights, outs = refs[:2], refs[2:-2], refs[-2:]
    for side in range(2):
        for tree in range(xs[0].shape[0]):
            for part, out in zip(picks, outs):
                out[side, tree] = project(xs[side], tree, part, weights)


def trunk_partial(mine, other, weights, **rest):
    trees, tok, _ = mine.shape
    arrays, picks = weights
    return call(
        functools.partial(partial_kernel, picks),
        "trunk_partial",
        [shape_of((2, trees, tok, arrays[0].shape[-1]), F32)] * 2,
        [mine, other, *arrays],
        [VMEM] * (2 + len(arrays)),
        **rest,
    )


def trunk_kernel(picks, mask, count, *refs):
    xs, earlier, weights = refs[:2], refs[2 : 2 + count], refs[2 + count : -6]
    low_ref, high_ref, first_ref, keys_ref, values_ref, state_ref = refs[-6:]
    top = (lax.axis_index("trunk") & mask) == 0
    trees, heads = state_ref.shape[1:3]
    low = low_ref.shape[1]
    for side in range(2):
        for tree in range(trees):
            keys, values = (project(xs[side], tree, part, weights) for part in picks)
            if earlier:
                keys, values = keys + earlier[0][side, tree], values + earlier[1][side, tree]
            keys, values = keys.astype(BF16), values.astype(BF16)
            keys_ref[side, tree] = keys
            values_ref[side, tree] = values
            for h in range(heads):
                at = slice(h * DH, (h + 1) * DH)
                state = lax.dot_general(
                    keys[:, at], values[:, at], (((0,), (0,)), ((), ())), preferred_element_type=F32
                )
                state_ref[side, tree, h] = state
                if side:
                    total = (state_ref[0, tree, h] + state).astype(BF16)
                    if h < low:
                        low_ref[tree, h] = total
                    else:
                        high_ref[tree, h - low] = total
                        first_ref[tree, h - low] = jnp.where(top, total, jnp.zeros_like(total))


def trunk_states(mine, other, weights, mask, earlier=(), **rest):
    trees, tok, width = mine.shape
    arrays, picks = weights
    cols = arrays[0].shape[-1]
    heads = cols // DH
    low = heads // 2
    return call(
        functools.partial(trunk_kernel, picks, mask, len(earlier)),
        "trunk_states",
        [
            shape_of((trees, low, DH, DH)),
            shape_of((trees, heads - low, DH, DH)),
            shape_of((trees, heads - low, DH, DH)),
            shape_of((2, trees, tok, cols)),
            shape_of((2, trees, tok, cols)),
            shape_of((2, trees, heads, DH, DH), F32),
        ],
        [mine, other, *earlier, *arrays],
        [VMEM] * (2 + len(earlier) + len(arrays)),
        **rest,
    )


def part_kernel(mine_ref, other_ref, keys_ref, values_ref, state_ref, fork_ref):
    core = core_index()
    tok = keys_ref.shape[2]
    entries, heads = fork_ref.shape[1:3]
    place = lax.broadcasted_iota(jnp.int32, (tok, DH), 0)
    for side in range(2):
        ints = other_ref if side else mine_ref
        for e in range(entries):
            tree = ints[1, e]
            inside = place < ints[0, e]
            odd = core != side
            for h in range(heads):
                at = slice(h * DH, (h + 1) * DH)
                keys = keys_ref[side, tree, :, at]
                part = lax.dot_general(
                    jnp.where(inside, keys, jnp.zeros_like(keys)),
                    values_ref[side, tree, :, at],
                    (((0,), (0,)), ((), ())),
                    preferred_element_type=F32,
                )
                lower = state_ref[1 - side, tree, h]
                fork_ref[side, e, h] = part + jnp.where(odd, lower, jnp.zeros_like(lower))


def fork_parts(forks, keys, values, states, **rest):
    _, _, tok, cols = keys.shape
    entries, heads = forks[0].shape[1], cols // DH
    return call(
        part_kernel,
        "fork_parts",
        [shape_of((2, entries, heads, DH, DH), F32)],
        [*forks, keys, values, states],
        [SMEM] * 2 + [VMEM] * 3,
        **rest,
    )


def scan_kernel(mask, low_ref, low_in_ref, high_ref, *refs):
    high_in, (low_out, high_out) = refs[:-2], refs[-2:]
    low_out[...] = (low_ref[...].astype(F32) + low_in_ref[...].astype(F32)).astype(BF16)
    total = jnp.where((lax.axis_index("trunk") & mask) == 0, high_ref[...].astype(F32), 0.0)
    for ref in high_in:
        total = total + ref[...].astype(F32)
    high_out[...] = total.astype(BF16)


def scan_step(low, low_in, high, high_in, mask, **rest):
    return call(
        functools.partial(scan_kernel, mask),
        "scan_step",
        [shape_of(low.shape), shape_of(high.shape)],
        [low, low_in, high, *high_in],
        [VMEM] * (3 + len(high_in)),
        **rest,
    )


def fork_kernel(low_masks, high_masks, lanes, *refs):
    ints, fork_ref, terms = refs[:2], refs[2], refs[3:]
    low_refs = terms[: len(low_masks)]
    high_refs = terms[len(low_masks) : len(low_masks) + len(high_masks)]
    outs, carried_ref = refs[-1 - lanes : -1], refs[-1]
    index, lane = lax.axis_index("trunk"), lax.axis_index("leaf")
    cap = outs[0].shape[1]
    first = 0
    for masks, terms in ((low_masks, low_refs), (high_masks, high_refs)):
        carried = None
        for mask, ref in zip(masks, terms):
            term = ref[...].astype(F32)
            if mask:
                term = jnp.where((index & mask) != 0, term, jnp.zeros_like(term))
            carried = term if carried is None else carried + term
        if terms:
            heads = terms[0].shape[1]
            carried_ref[:, first : first + heads] = carried
            first += heads
    for apart in range(lanes):
        for side in range(2):
            for c in range(cap):
                entry = (lane ^ apart) * cap + c
                state = fork_ref[side, entry] + carried_ref[ints[side][1, entry]]
                outs[apart][side, c] = state.astype(BF16)


def fork_states(forks, parts, low, high, lanes, **rest):
    _, entries, heads = parts.shape[:3]
    terms = [t for t, _ in low] + high
    trees = terms[0].shape[0]
    return call(
        functools.partial(fork_kernel, [m for _, m in low], [0] * len(high), lanes),
        "fork_states",
        [shape_of((2, entries // lanes, heads, DH, DH))] * lanes,
        [*forks, parts, *terms],
        [SMEM] * 2 + [VMEM] * (1 + len(terms)),
        scratch=[pltpu.VMEM((trees, heads, DH, DH), F32)],
        **rest,
    )


def branch_kernel(query_picks, by_lane, picks, count, blen, *refs):
    odd = lax.axis_index("leaf") % 2
    xs, query_refs, weights = refs[:2], refs[2 : 2 + count], refs[2 + count : -2]
    q_out, intra_out = refs[-2:]
    rows = xs[0].shape[1]
    row = lax.broadcasted_iota(jnp.int32, (rows, rows), 0)
    column = lax.broadcasted_iota(jnp.int32, (rows, rows), 1)
    seen = (column <= row) & (column >= row - lax.rem(row, blen))
    for side in range(2):
        for slot in range(xs[0].shape[0]):
            for i, part in enumerate(query_picks):
                q = project(xs[side], slot, part, query_refs).astype(BF16)
                place = (odd if i == 0 else 1 - odd) if by_lane else i
                first = pl.multiple_of(place * q.shape[1], q.shape[1])
                q_out[side, slot, :, pl.ds(first, q.shape[1])] = q
            k = project(xs[side], slot, picks[0], weights).astype(BF16)
            v = project(xs[side], slot, picks[1], weights).astype(BF16)
            for h in range(k.shape[1] // DH):
                at = slice(h * DH, (h + 1) * DH)
                scores = lax.dot_general(
                    q_out[side, slot, :, at],
                    k[:, at],
                    (((1,), (1,)), ((), ())),
                    preferred_element_type=F32,
                )
                scores = jnp.where(seen, scores, 0.0).astype(BF16)
                intra_out[side, slot, :, at] = dot(scores, v[:, at])


def branch_parts(mine, other, queries, by_lane, weights, **rest):
    slots, blen, width = mine.shape
    join = 2 if slots % 2 == 0 else 1
    mine, other = (a.reshape(slots // join, join * blen, width) for a in (mine, other))
    arrays = [*queries[0], *weights[0]]
    cols = weights[0][0].shape[-1]
    lead = (2, slots // join, join * blen, cols)
    outs = call(
        functools.partial(
            branch_kernel, queries[1], by_lane, weights[1], len(queries[0]), blen
        ),
        "branch_parts",
        [shape_of(lead), shape_of(lead, F32)],
        [mine, other, *arrays],
        [VMEM] * (2 + len(arrays)),
        **rest,
    )
    return [o.reshape(2, slots, blen, cols) for o in outs]


def norm_kernel(lanes, q_ref, intra_ref, *refs):
    states, outs = refs[:lanes], refs[lanes:]
    lane = lax.axis_index("leaf")
    cap, heads = states[0].shape[1:3]
    for apart in range(lanes):
        for side in range(2):
            for c in range(cap):
                slot = (lane ^ apart) * cap + c
                for h in range(heads):
                    at = slice(h * DH, (h + 1) * DH)
                    total = intra_ref[side, slot, :, at] + dot(
                        q_ref[side, slot, :, at], states[apart][side, c, h]
                    )
                    meansq = jnp.mean(total * total, axis=-1, keepdims=True)
                    normed = (total * lax.rsqrt(meansq + 1e-06)).astype(BF16)
                    if side == 0:
                        outs[0][slot, :, at] = normed
                    elif h < heads // 2:
                        outs[1][slot, :, at] = normed
                    else:
                        outs[2][slot, :, (h - heads // 2) * DH : (h - heads // 2 + 1) * DH] = normed


def norm_parts(queries, intra, states, **rest):
    _, slots, blen, cols = queries.shape
    return call(
        functools.partial(norm_kernel, len(states)),
        "norm_parts",
        [shape_of((slots, blen, w)) for w in (cols, cols // 2, cols // 2)],
        [queries, intra, *states],
        [VMEM] * (2 + len(states)),
        **rest,
    )


def place_kernel(picks, *refs):
    core, chip = core_index(), chip_index()
    sources, out_ref, sem = refs[:-2], refs[-2], refs[-1]
    copies = []
    for slot, number, index, offset in picks:
        source = sources[number].at[index] if index else sources[number]
        rows, half = source.shape
        first = (core if slot == 0 else 1 - core) * half
        target = out_ref.at[
            pl.ds(pl.multiple_of((chip ^ offset) * rows, rows), rows),
            pl.ds(pl.multiple_of(first, half), half),
        ]
        copies.append(pltpu.make_async_copy(source, target, sem.at[len(copies)]))
    for copy in copies:
        copy.start()
    for copy in copies:
        copy.wait()


def place_rows(weights, shape, **rest):
    arrays, picks = weights
    chosen = [(slot, *pick) for slot, part in enumerate(picks) for pick in part]
    return call(
        functools.partial(place_kernel, chosen),
        "place_rows",
        [shape_of(shape)],
        arrays,
        [ANY] * len(arrays),
        scratch=[pltpu.SemaphoreType.DMA((len(chosen),))],
        **rest,
    )[0]


def rows_of(w_ref, first, core, count):
    half = w_ref.shape[0] // 2
    return w_ref[pl.ds(pl.multiple_of(core * half + first, count), count), :]


def out_sum_kernel(first, terms, *refs):
    inputs, w_ref, out_ref = refs[: len(terms)], refs[len(terms)], refs[-1]
    core = core_index()
    slots, _, cols = inputs[0].shape
    weights = [rows_of(w_ref, f, core if own else 1 - core, cols) for f, own in terms]
    for slot in range(slots):
        total = refs[len(terms) + 1][slot] if first else None
        for ref, weight in zip(inputs, weights):
            term = dot(ref[slot], weight)
            total = term if total is None else total + term
        out_ref[slot] = total


def out_sum(inputs, terms, weights, total=None, **rest):
    slots, blen, cols = inputs[0].shape
    extra = [] if total is None else [total]
    return call(
        functools.partial(out_sum_kernel, total is not None, terms),
        "out_sum",
        [shape_of((slots, blen, weights.shape[1]), F32)],
        [*inputs, weights, *extra],
        [VMEM] * (len(inputs) + 1 + len(extra)),
        **rest,
    )[0]


def out_last_kernel(count, len_ref, *refs):
    inputs, (w_ref, total_ref, out_ref, held_ref, sem) = refs[:count], refs[count:]
    core = core_index()
    slots, blen, cols = inputs[0].shape
    weights = [rows_of(w_ref, i * cols, 1 - core, cols) for i in range(count)]
    row = lax.broadcasted_iota(jnp.int32, (blen, w_ref.shape[1]), 0)
    copies = []
    for slot in range(slots):
        total = total_ref[slot]
        for ref, weight in zip(inputs, weights):
            total = total + dot(ref[slot], weight)
        held_ref[slot] = jnp.where(row < len_ref[slot], total, 0.0).astype(BF16)
        copies.append(pltpu.make_async_copy(held_ref.at[slot], out_ref.at[slot], sem.at[slot]))
        copies[-1].start()
    for copy in copies:
        copy.wait()


def out_last(lengths, inputs, weights, total, **rest):
    slots, blen, _ = inputs[0].shape
    shape = (slots, blen, weights.shape[1])
    return call(
        functools.partial(out_last_kernel, len(inputs)),
        "out_last",
        [shape_of(shape)],
        [lengths, *inputs, weights, total],
        [SMEM] + [VMEM] * (2 + len(inputs)),
        [ANY],
        scratch=[pltpu.VMEM(shape, BF16), pltpu.SemaphoreType.DMA((slots,))],
        **rest,
    )[0]


def shards(
    trunk_tokens, branch_tokens, fork_offset, fork_tree, branch_len, w_query, w_key, w_value, w_out
):
    lanes, count = lax.axis_size("leaf"), lax.axis_size("trunk")
    bits = [1 << i for i in range(1, count.bit_length() - 1)]
    paired = len(bits) == 2 and lanes % 2 == 0 and (2 * w_key.shape[0]) % DH == 0
    order = []

    if paired:
        kv, qo = [w_key, w_value], [w_query, w_out]
        kv_other = [swap(w, "trunk", 1, "core") for w in kv]
        touch(kv, order=order)
        chosen = [(1, [(0, 0, True), (1, 0, True)])]
        (pair,) = chip_halves(kv, kv_other, chosen, order=order, weight=40.0)
        held = send_pair(pair, bits, "kv")
        qo_other = [swap(w, "trunk", 1, "core") for w in qo]
    own_forks = pack_forks(fork_offset, fork_tree, order=order)
    forks = (own_forks, swap(own_forks, "trunk", 1, "forks"))
    trunk_other = swap(trunk_tokens, "trunk", 1, "tokens")
    branch_other = swap(branch_tokens, "trunk", 1, "tokens")
    if paired:
        chosen = [
            (2, [(0, "even", True)]),
            (2, [(0, "odd", True)]),
            (1, [(1, 0, True), (1, 0, False)]),
        ]
        query, query_far, out_pair = chip_halves(
            qo, qo_other, chosen, order=order, landed=[forks[1]]
        )
        pair, _ = send_ahead(held, bits, "kv", order=order)
        arrays, picks = pair
        near = arrays[:3], [part[:3] for part in picks]
        *earlier, query = trunk_partial(
            trunk_tokens, trunk_other, near, order=order, through=[query], landed=[branch_other]
        )
        queries = send_across(query, query_far, bits, "query")
        last = arrays[3:], [[(n - 3, i, o) for n, i, o in part[3:]] for part in picks]
    else:
        pair = whole_pair([w_key, w_value], 1, [(0, 0), (1, 0)])
        queries = whole_pair([w_query], 2, [(0, 0), (0, 1)])
        out_full = lax.all_gather(w_out, "trunk", axis=0, tiled=True)
        earlier, last = (), pair

    low, high, message, *kept = trunk_states(
        trunk_tokens, trunk_other, last, bits[-1], earlier, order=order
    )
    low_terms, high_terms = [], []
    for step, (up, down) in enumerate(zip(bits, bits[::-1])):
        if step:
            low, message = scan_step(low, low_terms[-1][0], high, high_terms, down, order=order)
        low_terms.append((swap(low, "trunk", up, "scan"), up))
        high_terms.append(swap(message, "trunk", down, "scan"))
    (parts,) = fork_parts(forks, *kept, order=order)
    if paired:
        touch(queries[0][5:], order=order, weight=2.0)
    sends = fork_states(
        forks, parts, low_terms, high_terms, lanes, order=order,
        through=[out_pair] if paired else [],
    )
    far = sorted(range(1, lanes), key=lambda a: a == 1)
    moved = {a: swap(sends[a], "leaf", a, "lane") for a in far}
    received = [sends[0]] + [moved[a] for a in range(1, lanes)]
    if paired:
        held = send_pair(sends[lanes], bits, "out")
    q, intra = branch_parts(
        branch_tokens, branch_other, queries, paired, pair, order=order
    )
    if paired:
        outs, _ = send_ahead(held, bits, "out", order=order)
    mine, *other = norm_parts(q, intra, received, order=order)
    other = [swap(o, "trunk", 1, "normed") for o in other]
    if paired:
        out_full = place_rows(outs, (w_out.shape[0] * count, w_out.shape[1]), order=order)
    total = out_sum([mine], [(0, True)], out_full, order=order, weight=4.0)
    return out_last(branch_len, other, out_full, total, order=order)


def solution(mesh):
    in_specs = (
        P("leaf", "trunk", None),
        P(("leaf", "trunk"), None, None),
        P("leaf", "trunk", None),
        P("leaf", "trunk", None),
        P(("leaf", "trunk")),
        P("trunk", None),
        P("trunk", None),
        P("trunk", None),
        P("trunk", None),
    )
    out_specs = P(("leaf", "trunk"), None, None)
    return jax.shard_map(shards, mesh=mesh, in_specs=in_specs, out_specs=out_specs, check_vma=False)
```

```python
import functools

import jax
import jax.numpy as jnp
from jax import lax
from jax.experimental import pallas as pl
from jax.experimental.pallas import tpu as pltpu
from jax.sharding import PartitionSpec as P

H = 8
DH = 128
F32 = jnp.float32
BF16 = jnp.bfloat16
VMEM_BYTES = 16 * 1024 * 1024
ANY = pl.BlockSpec(memory_space=pl.ANY)
VMEM = pl.BlockSpec(memory_space=pltpu.VMEM)
SMEM = pl.BlockSpec(memory_space=pltpu.SMEM)


def swap(value, axis, bit, name="rows"):
    with jax.named_scope("to_" + name):
        return lax.ppermute(value, axis, [(i, i ^ bit) for i in range(lax.axis_size(axis))])


def turn(value, step, bits, name):
    bit = lambda i: bits[0] if (i % 2 == 1) == (step == 1) else bits[1]
    with jax.named_scope("to_" + name):
        count = lax.axis_size("trunk")
        return lax.ppermute(value, "trunk", [(i, i ^ bit(i)) for i in range(count)])


def dot(left, right):
    return jnp.dot(left, right, preferred_element_type=F32)


def shape_of(shape, dtype=BF16):
    return jax.ShapeDtypeStruct(tuple(shape), dtype)


def call(kernel, name, outs, inputs, specs, out_specs=None, scratch=(), order=None, through=(), landed=(), weight=0.0):
    after = (*(order or ()), *landed)
    n, t, w, m = len(inputs), len(through), len(after), len(outs)

    def body(*refs):
        kernel(*refs[:n], *refs[n + t + w : n + t + w + m], *refs[n + 2 * t + w + m :])

    results = pl.pallas_call(
        body,
        out_shape=[*outs, *(shape_of(a.shape, a.dtype) for a in through)],
        in_specs=[*specs, *[ANY] * (t + w)],
        out_specs=[*(out_specs or [VMEM] * m), *[ANY] * t],
        scratch_shapes=list(scratch),
        input_output_aliases={n + i: m + i for i in range(t)},
        compiler_params=pltpu.CompilerParams(vmem_limit_bytes=VMEM_BYTES),
        cost_estimate=pl.CostEstimate(
            flops=int(weight * 1e9), bytes_accessed=0, transcendentals=0
        ),
        name=name,
    )(*inputs, *through, *after)
    if order is not None:
        order[:] = [results[0]]
    return results


def core_index():
    return lax.axis_index("trunk") % 2


def chip_index():
    return lax.axis_index("trunk") // 2


def touch_kernel(*refs):
    refs[-1][...] = jnp.zeros_like(refs[-1])


def touch(arrays, **rest):
    return call(touch_kernel, "touch", [shape_of((8, DH), F32)], arrays, [ANY] * len(arrays), **rest)


def halves_kernel(count, chosen, *refs):
    core, odd = core_index(), lax.axis_index("leaf") % 2
    mine, other, outs, sem = refs[:count], refs[count : 2 * count], refs[2 * count : -1], refs[-1]
    copies = []
    for out, (parts, picks) in zip(outs, chosen):
        for slot, (i, p, own) in enumerate(picks):
            rows, width = other[i].shape
            part = width // 2 // parts
            p = {"even": odd, "odd": 1 - odd}.get(p, p)
            first = (core if own else 1 - core) * (width // 2) + p * part
            columns = pl.ds(pl.multiple_of(first, part), part)
            for source, place in ((mine[i], core), (other[i], 1 - core)):
                target = out.at[slot, pl.ds(pl.multiple_of(place * rows, rows), rows)]
                part_of = source if source.shape[1] == part else source.at[:, columns]
                copies.append(pltpu.make_async_copy(part_of, target, sem.at[len(copies)]))
    for copy in copies:
        copy.start()
    for copy in copies:
        copy.wait()


def chip_halves(mine, other, chosen, **rest):
    rows, width = other[0].shape
    return call(
        functools.partial(halves_kernel, len(mine), chosen),
        "chip_halves",
        [shape_of((len(picks), 2 * rows, width // 2 // parts)) for parts, picks in chosen],
        [*mine, *other],
        [ANY] * (2 * len(mine)),
        scratch=[pltpu.SemaphoreType.DMA((sum(2 * len(picks) for _, picks in chosen),))],
        **rest,
    )


def send_near(pair, bits, name):
    return [pair, *(turn(pair, step, bits, name) for step in (1, 2))]


def send_far(near, held, bits, name):
    arrays = [*near, turn(held, 2, bits, name + "_far")]
    return arrays, [[(i, (slot,), i) for i in range(4)] for slot in range(near[0].shape[0])]


def lane_pieces(near, far, other, across):
    arrays = [*near, far, other, *across]
    return arrays, [[(4 * i + k, (0,), k) for k in range(4)] for i in range(2)]


def whole_pair(weights, parts, chosen):
    arrays = []
    for i, p in chosen:
        full = lax.all_gather(weights[i], "trunk", axis=0, tiled=True)
        part = full.shape[1] // 2 // parts
        start = core_index() * (full.shape[1] // 2) + p * part
        arrays.append(lax.dynamic_slice_in_dim(full, start, part, axis=1))
    return arrays, [[(i, (), None)] for i in range(len(arrays))]


def chip_after(steps):
    first = jnp.where(core_index() == 1, 1, 2)
    return chip_index() ^ (0, first, 3 - first, 3)[steps]


def project(x_ref, lead, picks, refs):
    total = None
    for number, index, steps in picks:
        weight = refs[number][index] if index else refs[number][...]
        depth = weight.shape[0]
        if steps is None:
            left = x_ref[lead]
        else:
            left = x_ref[lead, :, pl.ds(pl.multiple_of(chip_after(steps) * depth, depth), depth)]
        term = dot(left, weight)
        total = term if total is None else total + term
    return total


def pack_kernel(offset_ref, tree_ref, out_ref):
    out_ref[0:1] = offset_ref[0]
    out_ref[1:2] = tree_ref[0]


def pack_forks(offset, tree, **rest):
    return call(
        pack_kernel,
        "pack_forks",
        [shape_of((2, offset.shape[2]), jnp.int32)],
        [offset, tree],
        [VMEM] * 2,
        **rest,
    )[0]


def partial_kernel(picks, *refs):
    xs, weights, outs = refs[:2], refs[2:-2], refs[-2:]
    for side in range(2):
        for tree in range(xs[0].shape[0]):
            for part, out in zip(picks, outs):
                out[side, tree] = project(xs[side], tree, part, weights)


def trunk_partial(mine, other, weights, **rest):
    trees, tok, _ = mine.shape
    arrays, picks = weights
    return call(
        functools.partial(partial_kernel, picks),
        "trunk_partial",
        [shape_of((2, trees, tok, arrays[0].shape[-1]), F32)] * 2,
        [mine, other, *arrays],
        [VMEM] * (2 + len(arrays)),
        **rest,
    )


def trunk_kernel(picks, mask, count, parts, *refs):
    xs, earlier, weights = refs[:2], refs[2 : 2 + count], refs[2 + count : -3 - 2 * parts]
    totals, firsts = refs[-3 - 2 * parts : -3 - parts], refs[-3 - parts : -3]
    keys_ref, values_ref, state_ref = refs[-3:]
    sent = (core_index() == 1) | ((lax.axis_index("trunk") & mask) == 0)
    trees, heads = state_ref.shape[1:3]
    for side in range(2):
        for tree in range(trees):
            keys, values = (project(xs[side], tree, part, weights) for part in picks)
            if earlier:
                keys, values = keys + earlier[0][side, tree], values + earlier[1][side, tree]
            keys, values = keys.astype(BF16), values.astype(BF16)
            keys_ref[side, tree] = keys
            values_ref[side, tree] = values
            for h in range(heads):
                at = slice(h * DH, (h + 1) * DH)
                state = lax.dot_general(
                    keys[:, at], values[:, at], (((0,), (0,)), ((), ())), preferred_element_type=F32
                )
                state_ref[side, tree, h] = state
                if side:
                    total = (state_ref[0, tree, h] + state).astype(BF16)
                    part, place = divmod(h, heads // parts)
                    totals[part][tree, place] = total
                    firsts[part][tree, place] = jnp.where(sent, total, jnp.zeros_like(total))


def trunk_states(mine, other, weights, mask, parts, earlier=(), **rest):
    trees, tok, width = mine.shape
    arrays, picks = weights
    cols = arrays[0].shape[-1]
    heads = cols // DH
    parts = parts if heads % parts == 0 else 1
    out = call(
        functools.partial(trunk_kernel, picks, mask, len(earlier), parts),
        "trunk_states",
        [
            *[shape_of((trees, heads // parts, DH, DH))] * (2 * parts),
            shape_of((2, trees, tok, cols)),
            shape_of((2, trees, tok, cols)),
            shape_of((2, trees, heads, DH, DH), F32),
        ],
        [mine, other, *earlier, *arrays],
        [VMEM] * (2 + len(earlier) + len(arrays)),
        **rest,
    )
    return out[:parts], out[parts : 2 * parts], out[2 * parts :]


def part_kernel(mine_ref, other_ref, keys_ref, values_ref, state_ref, fork_ref):
    core = core_index()
    tok = keys_ref.shape[2]
    entries, heads = fork_ref.shape[1:3]
    place = lax.broadcasted_iota(jnp.int32, (tok, DH), 0)
    for side in range(2):
        ints = other_ref if side else mine_ref
        for e in range(entries):
            tree = ints[1, e]
            inside = place < ints[0, e]
            odd = core != side
            for h in range(heads):
                at = slice(h * DH, (h + 1) * DH)
                keys = keys_ref[side, tree, :, at]
                part = lax.dot_general(
                    jnp.where(inside, keys, jnp.zeros_like(keys)),
                    values_ref[side, tree, :, at],
                    (((0,), (0,)), ((), ())),
                    preferred_element_type=F32,
                )
                lower = state_ref[1 - side, tree, h]
                fork_ref[side, e, h] = part + jnp.where(odd, lower, jnp.zeros_like(lower))


def fork_parts(forks, keys, values, states, **rest):
    _, _, tok, cols = keys.shape
    entries, heads = forks[0].shape[1], cols // DH
    return call(
        part_kernel,
        "fork_parts",
        [shape_of((2, entries, heads, DH, DH), F32)],
        [*forks, keys, values, states],
        [SMEM] * 2 + [VMEM] * 3,
        **rest,
    )


def scan_kernel(mask, count, *refs):
    adds = (core_index() == 1) | ((lax.axis_index("trunk") & mask) == 0)
    for held_ref, in_ref, out_ref in zip(refs[:count], refs[count : 2 * count], refs[2 * count :]):
        held = held_ref[...].astype(F32)
        if mask:
            held = jnp.where(adds, held, jnp.zeros_like(held))
        out_ref[...] = (held + in_ref[...].astype(F32)).astype(BF16)


def scan_step(held, received, mask, **rest):
    return call(
        functools.partial(scan_kernel, mask, len(held)),
        "scan_step",
        [shape_of(h.shape) for h in held],
        [*held, *received],
        [VMEM] * (2 * len(held)),
        **rest,
    )


def fork_kernel(masks, both, lanes, parts, *refs):
    count = len(masks) * parts
    ints, fork_ref, terms = refs[:2], refs[2], refs[3 : 3 + count]
    outs, carried_ref = refs[-1 - lanes : -1], refs[-1]
    index, lane = lax.axis_index("trunk"), lax.axis_index("leaf")
    cap = outs[0].shape[1]
    heads = terms[0].shape[1]
    for part in range(parts):
        carried = None
        for mask, ref in zip(masks, terms[part::parts]):
            term = ref[...].astype(F32)
            counts = (index & mask) != 0
            if both:
                counts = counts | (core_index() == 0)
            term = jnp.where(counts, term, jnp.zeros_like(term))
            carried = term if carried is None else carried + term
        carried_ref[:, part * heads : (part + 1) * heads] = carried
    for apart in range(lanes):
        for side in range(2):
            for c in range(cap):
                entry = (lane ^ apart) * cap + c
                state = fork_ref[side, entry] + carried_ref[ints[side][1, entry]]
                outs[apart][side, c] = state.astype(BF16)


def fork_states(forks, parts, terms, masks, both, lanes, **rest):
    _, entries, heads = parts.shape[:3]
    shape = (2, entries // lanes, heads, DH, DH)
    return call(
        functools.partial(fork_kernel, masks, both, lanes, len(terms[0])),
        "fork_states",
        [shape_of(shape)] * lanes,
        [*forks, parts, *(t for term in terms for t in term)],
        [SMEM] * 2 + [VMEM] * (1 + len(terms) * len(terms[0])),
        scratch=[pltpu.VMEM((terms[0][0].shape[0], heads, DH, DH), F32)],
        **rest,
    )


def branch_kernel(counts, picks, by_lane, blen, *refs):
    odd = lax.axis_index("leaf") % 2
    xs, q_out, intra_out = refs[:2], *refs[-2:]
    query_refs, weights = refs[2 : 2 + counts[0]], refs[2 + counts[0] : -2]
    rows = xs[0].shape[1]
    row = lax.broadcasted_iota(jnp.int32, (rows, rows), 0)
    column = lax.broadcasted_iota(jnp.int32, (rows, rows), 1)
    seen = (column <= row) & (column >= row - lax.rem(row, blen))
    for side in range(2):
        for slot in range(xs[0].shape[0]):
            for i, part in enumerate(picks[0]):
                q = project(xs[side], slot, part, query_refs).astype(BF16)
                place = (odd if i == 0 else 1 - odd) if by_lane else i
                first = pl.multiple_of(place * q.shape[1], q.shape[1])
                q_out[side, slot, :, pl.ds(first, q.shape[1])] = q
            k, v = (project(xs[side], slot, part, weights).astype(BF16) for part in picks[1])
            for h in range(k.shape[1] // DH):
                at = slice(h * DH, (h + 1) * DH)
                scores = lax.dot_general(
                    q_out[side, slot, :, at],
                    k[:, at],
                    (((1,), (1,)), ((), ())),
                    preferred_element_type=F32,
                )
                scores = jnp.where(seen, scores, 0.0).astype(BF16)
                intra_out[side, slot, :, at] = dot(scores, v[:, at])


def branch_parts(mine, other, queries, pair, by_lane, **rest):
    slots, blen, width = mine.shape
    join = 2 if slots % 2 == 0 else 1
    mine, other = (a.reshape(slots // join, join * blen, width) for a in (mine, other))
    weights = [queries, pair]
    arrays = [a for held, _ in weights for a in held]
    cols = pair[0][0].shape[-1]
    lead = (2, slots // join, join * blen, cols)
    outs = call(
        functools.partial(
            branch_kernel, [len(held) for held, _ in weights], [p for _, p in weights], by_lane, blen
        ),
        "branch_parts",
        [shape_of(lead), shape_of(lead, F32)],
        [mine, other, *arrays],
        [VMEM] * (2 + len(arrays)),
        **rest,
    )
    return [o.reshape(2, slots, blen, cols) for o in outs]


def norm_kernel(aparts, q_ref, intra_ref, *refs):
    states, outs = refs[: len(aparts)], refs[len(aparts) :]
    lane = lax.axis_index("leaf")
    cap, heads = states[0].shape[1:3]
    for number, apart in enumerate(aparts):
        for side in range(2):
            for c in range(cap):
                slot = (lane ^ apart) * cap + c
                for h in range(heads):
                    at = slice(h * DH, (h + 1) * DH)
                    total = intra_ref[side, slot, :, at] + dot(
                        q_ref[side, slot, :, at], states[number][side, c, h]
                    )
                    meansq = jnp.mean(total * total, axis=-1, keepdims=True)
                    normed = (total * lax.rsqrt(meansq + 1e-06)).astype(BF16)
                    outs[side][number * cap + c, :, at] = normed


def norm_parts(queries, intra, states, aparts, **rest):
    _, _, blen, cols = queries.shape
    count = len(aparts) * states[0].shape[1]
    return call(
        functools.partial(norm_kernel, aparts),
        "norm_parts",
        [shape_of((count, blen, cols))] * 2,
        [queries, intra, *(states[a] for a in aparts)],
        [VMEM] * (2 + len(aparts)),
        **rest,
    )


def place_kernel(picks, *refs):
    core = core_index()
    sources, out_ref, sem = refs[:-2], refs[-2], refs[-1]
    copies = []
    for slot, number, index, steps in picks:
        source = sources[number].at[index] if index else sources[number]
        rows, half = source.shape
        first = (core if slot == 0 else 1 - core) * half
        target = out_ref.at[
            pl.ds(pl.multiple_of(chip_after(steps) * rows, rows), rows),
            pl.ds(pl.multiple_of(first, half), half),
        ]
        copies.append(pltpu.make_async_copy(source, target, sem.at[len(copies)]))
    for copy in copies:
        copy.start()
    for copy in copies:
        copy.wait()


def place_rows(weights, shape, **rest):
    arrays, picks = weights
    chosen = [(slot, *pick) for slot, part in enumerate(picks) for pick in part]
    return call(
        functools.partial(place_kernel, chosen),
        "place_rows",
        [shape_of(shape)],
        arrays,
        [ANY] * len(arrays),
        scratch=[pltpu.SemaphoreType.DMA((len(chosen),))],
        **rest,
    )[0]


def rows_of(w_ref, first, core, count):
    half = w_ref.shape[0] // 2
    return w_ref[pl.ds(pl.multiple_of(core * half + first, count), count), :]


def out_sum_kernel(*refs):
    inputs, w_ref, out_ref = refs[:-2], refs[-2], refs[-1]
    weight = rows_of(w_ref, 0, core_index(), inputs[0].shape[2])
    first = 0
    for ref in inputs:
        slots, blen, cols = ref.shape
        out_ref[first : first + slots * blen] = dot(ref[...].reshape(slots * blen, cols), weight)
        first += slots * blen


def out_sum(normed, weights, **rest):
    rows = sum(n.shape[0] * n.shape[1] for n in normed)
    return call(
        out_sum_kernel,
        "out_sum",
        [shape_of((rows, weights.shape[1]), F32)],
        [*normed, weights],
        [VMEM] * (len(normed) + 1),
        **rest,
    )[0]


def out_last_kernel(aparts, cap, len_ref, *refs):
    inputs, (w_ref, total_ref, out_ref, held_ref, sem) = refs[:-5], refs[-5:]
    weight = rows_of(w_ref, 0, 1 - core_index(), inputs[0].shape[2])
    lane = lax.axis_index("leaf")
    blen = inputs[0].shape[1]
    row = lax.broadcasted_iota(jnp.int32, (blen, w_ref.shape[1]), 0)
    copies, place = [], 0
    for ref in inputs:
        count = ref.shape[0]
        rows = slice(place * blen, (place + count) * blen)
        total = total_ref[rows] + dot(ref[...].reshape(count * blen, ref.shape[2]), weight)
        for i in range(count):
            slot = (lane ^ aparts[place // cap]) * cap + place % cap
            part = total[i * blen : (i + 1) * blen]
            held_ref[place] = jnp.where(row < len_ref[slot], part, 0.0).astype(BF16)
            copies.append(pltpu.make_async_copy(held_ref.at[place], out_ref.at[slot], sem.at[place]))
            copies[-1].start()
            place += 1
    for copy in copies:
        copy.wait()


def out_last(lengths, normed, aparts, weights, total, **rest):
    slots, blen = lengths.shape[0], normed[0].shape[1]
    shape = (slots, blen, weights.shape[1])
    return call(
        functools.partial(out_last_kernel, aparts, slots // len(aparts)),
        "out_last",
        [shape_of(shape)],
        [lengths, *normed, weights, total],
        [SMEM] + [VMEM] * (2 + len(normed)),
        [ANY],
        scratch=[pltpu.VMEM(shape, BF16), pltpu.SemaphoreType.DMA((slots,))],
        **rest,
    )[0]


def shards(
    trunk_tokens, branch_tokens, fork_offset, fork_tree, branch_len, w_query, w_key, w_value, w_out
):
    lanes, count = lax.axis_size("leaf"), lax.axis_size("trunk")
    bits = [1 << i for i in range(1, count.bit_length() - 1)]
    paired = len(bits) == 2 and lanes % 2 == 0 and (2 * w_key.shape[0]) % DH == 0
    order = []
    chain = functools.partial(touch, order=order)

    if paired:
        kv, qo = [w_key, w_value], [w_query, w_out]
        kv_other = [swap(w, "trunk", 1, "core") for w in kv]
        half = w_key.shape[1] // 2
        kv = [lax.dynamic_slice_in_dim(w, core_index() * half, half, axis=1) for w in kv]
        chain(kv)
        chosen = [(1, [(0, 0, True), (1, 0, True)])]
        (own_kv,) = chip_halves(kv, kv_other, chosen, order=order, weight=40.0)
        near = send_near(own_kv, bits, "kv")
        qo_other = [swap(w, "trunk", 1, "core") for w in qo]
    own_forks = pack_forks(fork_offset, fork_tree, order=order)
    forks = (own_forks, swap(own_forks, "trunk", 1, "forks"))
    trunk_other = swap(trunk_tokens, "trunk", 1, "tokens")
    branch_other = swap(branch_tokens, "trunk", 1, "tokens")
    trunk = trunk_tokens, trunk_other
    if paired:
        chosen = [
            (2, [(0, "even", True)]),
            (2, [(0, "odd", True)]),
            (1, [(1, 0, True), (1, 0, False)]),
            (1, [(1, 0, True), (1, 0, False)]),
        ]
        own_q, other_q, own_o, again_o = chip_halves(qo, qo_other, chosen, order=order, landed=[forks[1]])
        _, near[1] = chain([], through=[near[1]])
        arrays, picks = pair = send_far(near, near[1], bits, "kv")
        at_hand = arrays[:3], [part[:3] for part in picks]
        earlier = trunk_partial(*trunk, at_hand, order=order, landed=[branch_other])
        _, own_q = chain(arrays[3:], through=[own_q])
        near_q = send_near(own_q, bits, "query")
        last = arrays[3:], [[(0, i, steps) for _, i, steps in part[3:]] for part in picks]
    else:
        pair = whole_pair([w_key, w_value], 1, [(0, 0), (1, 0)])
        queries = whole_pair([w_query], 2, [(0, 0), (0, 1)])
        out_full = lax.all_gather(w_out, "trunk", axis=0, tiled=True)
        earlier, last = (), pair

    def scan_round(held, number):
        if paired:
            return [turn(h, 1 + number, bits, "scan") for h in held]
        return [swap(h, "trunk", bits[number]) for h in held]

    mask = bits[1] if paired else 0
    held, first, kept = trunk_states(*trunk, last, mask, 1, earlier, order=order)
    terms = [scan_round(first, 0)]
    if paired:
        _, near_q[1] = chain(near_q[2:], through=[near_q[1]], weight=5.0)
        far_q = turn(near_q[1], 2, bits, "query_far")
        across = [swap(a, "leaf", 1, "query_lane") for a in near_q[1:]]
    for number in range(1, len(bits)):
        held = scan_step(held, terms[-1], bits[0] if paired else 0, order=order)
        terms.append(scan_round(held, number))
    if paired:
        _, far_q = chain([], through=[far_q])
        last_q = swap(far_q, "leaf", 1, "query_lane")
        queries = lane_pieces(near_q, far_q, other_q, [*across, last_q])
    (parts,) = fork_parts(forks, *kept, order=order)
    if paired:
        chain(across, weight=6.0)
    sends = fork_states(
        forks, parts, terms, bits, paired, lanes, order=order, through=[own_o] if paired else []
    )
    far = sorted(range(1, lanes), key=lambda a: a == 1)
    moved = {a: swap(sends[a], "leaf", a, "lane") for a in far}
    received = [sends[0]] + [moved[a] for a in range(1, lanes)]
    if paired:
        held_o = turn(sends[lanes], 1, bits, "out")
        _, again_o = chain([last_q], through=[again_o])
        near_o = [again_o, held_o, turn(again_o, 2, bits, "out")]
    q, intra = branch_parts(
        branch_tokens, branch_other, queries, pair, paired, order=order, weight=20.0
    )
    if paired:
        _, near_o[1] = chain([], through=[held_o])
        outs = send_far(near_o, near_o[1], bits, "out")
    aparts = list(range(lanes))
    split = [aparts[:-1], aparts[-1:]] if lanes > 1 else [aparts]
    mine, other = [], []
    for part in split:
        if mine and paired:
            chain(near_o[2:3], weight=1.0)
        own, theirs = norm_parts(q, intra, received, part, order=order, weight=4.0 if mine else 0.5)
        mine.append(own)
        other.append(swap(theirs, "trunk", 1, "normed"))
    if paired:
        chain(other[:1])
        out_full = place_rows(
            outs, (w_out.shape[0] * count, w_out.shape[1]), order=order, weight=8.0
        )
    total = out_sum(mine, out_full, order=order)
    return out_last(branch_len, other, aparts, out_full, total, order=order)


def solution(mesh):
    in_specs = (
        P("leaf", "trunk", None),
        P(("leaf", "trunk"), None, None),
        P("leaf", "trunk", None),
        P("leaf", "trunk", None),
        P(("leaf", "trunk")),
        P("trunk", None),
        P("trunk", None),
        P("trunk", None),
        P("trunk", None),
    )
    out_specs = P(("leaf", "trunk"), None, None)
    return jax.shard_map(shards, mesh=mesh, in_specs=in_specs, out_specs=out_specs, check_vma=False)
```

```python
import functools

import jax
import jax.numpy as jnp
from jax import lax
from jax.experimental import pallas as pl
from jax.experimental.pallas import tpu as pltpu
from jax.sharding import PartitionSpec as P

H = 8
DH = 128
F32 = jnp.float32
BF16 = jnp.bfloat16
VMEM_BYTES = 16 * 1024 * 1024
ANY = pl.BlockSpec(memory_space=pl.ANY)
VMEM = pl.BlockSpec(memory_space=pltpu.VMEM)
SMEM = pl.BlockSpec(memory_space=pltpu.SMEM)


def swap(value, axis, bit, name="rows"):
    with jax.named_scope("to_" + name):
        return lax.ppermute(value, axis, [(i, i ^ bit) for i in range(lax.axis_size(axis))])


def turn(value, step, bits, name):
    bit = lambda i: bits[0] if (i % 2 == 1) == (step == 1) else bits[1]
    with jax.named_scope("to_" + name):
        count = lax.axis_size("trunk")
        return lax.ppermute(value, "trunk", [(i, i ^ bit(i)) for i in range(count)])


def dot(left, right):
    return jnp.dot(left, right, preferred_element_type=F32)


def shape_of(shape, dtype=BF16):
    return jax.ShapeDtypeStruct(tuple(shape), dtype)


def call(kernel, name, outs, inputs, specs, out_specs=None, scratch=(), order=None, through=(), landed=(), weight=0.0):
    after = (*(order or ()), *landed)
    n, t, w, m = len(inputs), len(through), len(after), len(outs)

    def body(*refs):
        kernel(*refs[:n], *refs[n + t + w : n + t + w + m], *refs[n + 2 * t + w + m :])

    results = pl.pallas_call(
        body,
        out_shape=[*outs, *(shape_of(a.shape, a.dtype) for a in through)],
        in_specs=[*specs, *[ANY] * (t + w)],
        out_specs=[*(out_specs or [VMEM] * m), *[ANY] * t],
        scratch_shapes=list(scratch),
        input_output_aliases={n + i: m + i for i in range(t)},
        compiler_params=pltpu.CompilerParams(vmem_limit_bytes=VMEM_BYTES),
        cost_estimate=pl.CostEstimate(
            flops=int(weight * 1e9), bytes_accessed=0, transcendentals=0
        ),
        name=name,
    )(*inputs, *through, *after)
    if order is not None:
        order[:] = [results[0]]
    return results


def core_index():
    return lax.axis_index("trunk") % 2


def chip_index():
    return lax.axis_index("trunk") // 2


def touch_kernel(*refs):
    refs[-1][...] = jnp.zeros_like(refs[-1])


def touch(arrays, **rest):
    return call(touch_kernel, "touch", [shape_of((8, DH), F32)], arrays, [ANY] * len(arrays), **rest)


def halves_kernel(count, chosen, *refs):
    core, odd = core_index(), lax.axis_index("leaf") % 2
    mine, other, outs, sem = refs[:count], refs[count : 2 * count], refs[2 * count : -1], refs[-1]
    copies = []
    for out, (parts, picks) in zip(outs, chosen):
        for slot, (i, p, own) in enumerate(picks):
            rows, width = other[i].shape
            part = width // 2 // parts
            p = {"even": odd, "odd": 1 - odd}.get(p, p)
            first = (core if own else 1 - core) * (width // 2) + p * part
            columns = pl.ds(pl.multiple_of(first, part), part)
            for source, place in ((mine[i], core), (other[i], 1 - core)):
                target = out.at[slot, pl.ds(pl.multiple_of(place * rows, rows), rows)]
                part_of = source if source.shape[1] == part else source.at[:, columns]
                copies.append(pltpu.make_async_copy(part_of, target, sem.at[len(copies)]))
    for copy in copies:
        copy.start()
    for copy in copies:
        copy.wait()


def chip_halves(mine, other, chosen, **rest):
    rows, width = other[0].shape
    return call(
        functools.partial(halves_kernel, len(mine), chosen),
        "chip_halves",
        [shape_of((len(picks), 2 * rows, width // 2 // parts)) for parts, picks in chosen],
        [*mine, *other],
        [ANY] * (2 * len(mine)),
        scratch=[pltpu.SemaphoreType.DMA((sum(2 * len(picks) for _, picks in chosen),))],
        **rest,
    )


def send_near(pair, bits, name):
    return [pair, *(turn(pair, step, bits, name) for step in (1, 2))]


def send_far(near, held, bits, name):
    arrays = [*near, turn(held, 2, bits, name + "_far")]
    return arrays, [[(i, (slot,), i) for i in range(4)] for slot in range(near[0].shape[0])]


def lane_pieces(near, far, other, across):
    arrays = [*near, far, other, *across]
    return arrays, [[(4 * i + k, (0,), k) for k in range(4)] for i in range(2)]


def whole_pair(weights, parts, chosen):
    arrays = []
    for i, p in chosen:
        full = lax.all_gather(weights[i], "trunk", axis=0, tiled=True)
        part = full.shape[1] // 2 // parts
        start = core_index() * (full.shape[1] // 2) + p * part
        arrays.append(lax.dynamic_slice_in_dim(full, start, part, axis=1))
    return arrays, [[(i, (), None)] for i in range(len(arrays))]


def chip_after(steps):
    first = jnp.where(core_index() == 1, 1, 2)
    return chip_index() ^ (0, first, 3 - first, 3)[steps]


def project(x_ref, lead, picks, refs):
    total = None
    for number, index, steps in picks:
        weight = refs[number][index] if index else refs[number][...]
        depth = weight.shape[0]
        if steps is None:
            left = x_ref[lead]
        else:
            left = x_ref[lead, :, pl.ds(pl.multiple_of(chip_after(steps) * depth, depth), depth)]
        term = dot(left, weight)
        total = term if total is None else total + term
    return total


def pack_kernel(offset_ref, tree_ref, out_ref):
    out_ref[0:1] = offset_ref[0]
    out_ref[1:2] = tree_ref[0]


def pack_forks(offset, tree, **rest):
    return call(
        pack_kernel,
        "pack_forks",
        [shape_of((2, offset.shape[2]), jnp.int32)],
        [offset, tree],
        [VMEM] * 2,
        **rest,
    )[0]


def partial_kernel(picks, *refs):
    xs, weights, outs = refs[:2], refs[2:-2], refs[-2:]
    for side in range(2):
        for tree in range(xs[0].shape[0]):
            for part, out in zip(picks, outs):
                out[side, tree] = project(xs[side], tree, part, weights)


def trunk_partial(mine, other, weights, **rest):
    trees, tok, _ = mine.shape
    arrays, picks = weights
    return call(
        functools.partial(partial_kernel, picks),
        "trunk_partial",
        [shape_of((2, trees, tok, arrays[0].shape[-1]), F32)] * 2,
        [mine, other, *arrays],
        [VMEM] * (2 + len(arrays)),
        **rest,
    )


def trunk_kernel(picks, mask, count, parts, *refs):
    xs, earlier, weights = refs[:2], refs[2 : 2 + count], refs[2 + count : -3 - 2 * parts]
    totals, firsts = refs[-3 - 2 * parts : -3 - parts], refs[-3 - parts : -3]
    keys_ref, values_ref, state_ref = refs[-3:]
    sent = (core_index() == 1) | ((lax.axis_index("trunk") & mask) == 0)
    trees, heads = state_ref.shape[1:3]
    for side in range(2):
        for tree in range(trees):
            keys, values = (project(xs[side], tree, part, weights) for part in picks)
            if earlier:
                keys, values = keys + earlier[0][side, tree], values + earlier[1][side, tree]
            keys, values = keys.astype(BF16), values.astype(BF16)
            keys_ref[side, tree] = keys
            values_ref[side, tree] = values
            for h in range(heads):
                at = slice(h * DH, (h + 1) * DH)
                state = lax.dot_general(
                    keys[:, at], values[:, at], (((0,), (0,)), ((), ())), preferred_element_type=F32
                )
                state_ref[side, tree, h] = state
                if side:
                    total = (state_ref[0, tree, h] + state).astype(BF16)
                    part, place = divmod(h, heads // parts)
                    totals[part][tree, place] = total
                    firsts[part][tree, place] = jnp.where(sent, total, jnp.zeros_like(total))


def trunk_states(mine, other, weights, mask, parts, earlier=(), **rest):
    trees, tok, width = mine.shape
    arrays, picks = weights
    cols = arrays[0].shape[-1]
    heads = cols // DH
    parts = parts if heads % parts == 0 else 1
    out = call(
        functools.partial(trunk_kernel, picks, mask, len(earlier), parts),
        "trunk_states",
        [
            *[shape_of((trees, heads // parts, DH, DH))] * (2 * parts),
            shape_of((2, trees, tok, cols)),
            shape_of((2, trees, tok, cols)),
            shape_of((2, trees, heads, DH, DH), F32),
        ],
        [mine, other, *earlier, *arrays],
        [VMEM] * (2 + len(earlier) + len(arrays)),
        **rest,
    )
    return out[:parts], out[parts : 2 * parts], out[2 * parts :]


def part_kernel(mine_ref, other_ref, keys_ref, values_ref, state_ref, fork_ref):
    core = core_index()
    tok = keys_ref.shape[2]
    entries, heads = fork_ref.shape[1:3]
    place = lax.broadcasted_iota(jnp.int32, (tok, DH), 0)
    for side in range(2):
        ints = other_ref if side else mine_ref
        for e in range(entries):
            tree = ints[1, e]
            inside = place < ints[0, e]
            odd = core != side
            for h in range(heads):
                at = slice(h * DH, (h + 1) * DH)
                keys = keys_ref[side, tree, :, at]
                part = lax.dot_general(
                    jnp.where(inside, keys, jnp.zeros_like(keys)),
                    values_ref[side, tree, :, at],
                    (((0,), (0,)), ((), ())),
                    preferred_element_type=F32,
                )
                lower = state_ref[1 - side, tree, h]
                fork_ref[side, e, h] = part + jnp.where(odd, lower, jnp.zeros_like(lower))


def fork_parts(forks, keys, values, states, **rest):
    _, _, tok, cols = keys.shape
    entries, heads = forks[0].shape[1], cols // DH
    return call(
        part_kernel,
        "fork_parts",
        [shape_of((2, entries, heads, DH, DH), F32)],
        [*forks, keys, values, states],
        [SMEM] * 2 + [VMEM] * 3,
        **rest,
    )


def scan_kernel(mask, count, *refs):
    adds = (core_index() == 1) | ((lax.axis_index("trunk") & mask) == 0)
    for held_ref, in_ref, out_ref in zip(refs[:count], refs[count : 2 * count], refs[2 * count :]):
        held = held_ref[...].astype(F32)
        if mask:
            held = jnp.where(adds, held, jnp.zeros_like(held))
        out_ref[...] = (held + in_ref[...].astype(F32)).astype(BF16)


def scan_step(held, received, mask, **rest):
    return call(
        functools.partial(scan_kernel, mask, len(held)),
        "scan_step",
        [shape_of(h.shape) for h in held],
        [*held, *received],
        [VMEM] * (2 * len(held)),
        **rest,
    )


def fork_kernel(masks, both, lanes, parts, *refs):
    count = len(masks) * parts
    ints, fork_ref, terms = refs[:2], refs[2], refs[3 : 3 + count]
    outs, carried_ref = refs[-1 - lanes : -1], refs[-1]
    index, lane = lax.axis_index("trunk"), lax.axis_index("leaf")
    cap = outs[0].shape[1]
    heads = terms[0].shape[1]
    for part in range(parts):
        carried = None
        for mask, ref in zip(masks, terms[part::parts]):
            term = ref[...].astype(F32)
            counts = (index & mask) != 0
            if both:
                counts = counts | (core_index() == 0)
            term = jnp.where(counts, term, jnp.zeros_like(term))
            carried = term if carried is None else carried + term
        carried_ref[:, part * heads : (part + 1) * heads] = carried
    for apart in range(lanes):
        for side in range(2):
            for c in range(cap):
                entry = (lane ^ apart) * cap + c
                state = fork_ref[side, entry] + carried_ref[ints[side][1, entry]]
                outs[apart][side, c] = state.astype(BF16)


def fork_states(forks, parts, terms, masks, both, lanes, **rest):
    _, entries, heads = parts.shape[:3]
    shape = (2, entries // lanes, heads, DH, DH)
    return call(
        functools.partial(fork_kernel, masks, both, lanes, len(terms[0])),
        "fork_states",
        [shape_of(shape)] * lanes,
        [*forks, parts, *(t for term in terms for t in term)],
        [SMEM] * 2 + [VMEM] * (1 + len(terms) * len(terms[0])),
        scratch=[pltpu.VMEM((terms[0][0].shape[0], heads, DH, DH), F32)],
        **rest,
    )


def branch_kernel(counts, picks, by_lane, blen, *refs):
    odd = lax.axis_index("leaf") % 2
    xs, q_out, intra_out = refs[:2], *refs[-2:]
    query_refs, weights = refs[2 : 2 + counts[0]], refs[2 + counts[0] : -2]
    rows = xs[0].shape[1]
    row = lax.broadcasted_iota(jnp.int32, (rows, rows), 0)
    column = lax.broadcasted_iota(jnp.int32, (rows, rows), 1)
    seen = (column <= row) & (column >= row - lax.rem(row, blen))
    for side in range(2):
        for slot in range(xs[0].shape[0]):
            for i, part in enumerate(picks[0]):
                q = project(xs[side], slot, part, query_refs).astype(BF16)
                place = (odd if i == 0 else 1 - odd) if by_lane else i
                first = pl.multiple_of(place * q.shape[1], q.shape[1])
                q_out[side, slot, :, pl.ds(first, q.shape[1])] = q
            k, v = (project(xs[side], slot, part, weights).astype(BF16) for part in picks[1])
            for h in range(k.shape[1] // DH):
                at = slice(h * DH, (h + 1) * DH)
                scores = lax.dot_general(
                    q_out[side, slot, :, at],
                    k[:, at],
                    (((1,), (1,)), ((), ())),
                    preferred_element_type=F32,
                )
                scores = jnp.where(seen, scores, 0.0).astype(BF16)
                intra_out[side, slot, :, at] = dot(scores, v[:, at])


def branch_parts(mine, other, queries, pair, by_lane, **rest):
    slots, blen, width = mine.shape
    join = 2 if slots % 2 == 0 else 1
    mine, other = (a.reshape(slots // join, join * blen, width) for a in (mine, other))
    weights = [queries, pair]
    arrays = [a for held, _ in weights for a in held]
    cols = pair[0][0].shape[-1]
    lead = (2, slots // join, join * blen, cols)
    outs = call(
        functools.partial(
            branch_kernel, [len(held) for held, _ in weights], [p for _, p in weights], by_lane, blen
        ),
        "branch_parts",
        [shape_of(lead), shape_of(lead, F32)],
        [mine, other, *arrays],
        [VMEM] * (2 + len(arrays)),
        **rest,
    )
    return [o.reshape(2, slots, blen, cols) for o in outs]


def norm_kernel(aparts, q_ref, intra_ref, *refs):
    states, outs = refs[: len(aparts)], refs[len(aparts) :]
    lane = lax.axis_index("leaf")
    cap, heads = states[0].shape[1:3]
    for number, apart in enumerate(aparts):
        for side in range(2):
            for c in range(cap):
                slot = (lane ^ apart) * cap + c
                for h in range(heads):
                    at = slice(h * DH, (h + 1) * DH)
                    total = intra_ref[side, slot, :, at] + dot(
                        q_ref[side, slot, :, at], states[number][side, c, h]
                    )
                    meansq = jnp.mean(total * total, axis=-1, keepdims=True)
                    normed = (total * lax.rsqrt(meansq + 1e-06)).astype(BF16)
                    outs[side][number * cap + c, :, at] = normed


def norm_parts(queries, intra, states, aparts, **rest):
    _, _, blen, cols = queries.shape
    count = len(aparts) * states[0].shape[1]
    return call(
        functools.partial(norm_kernel, aparts),
        "norm_parts",
        [shape_of((count, blen, cols))] * 2,
        [queries, intra, *(states[a] for a in aparts)],
        [VMEM] * (2 + len(aparts)),
        **rest,
    )


def place_kernel(picks, *refs):
    core = core_index()
    sources, out_ref, sem = refs[:-2], refs[-2], refs[-1]
    copies = []
    for slot, number, index, steps in picks:
        source = sources[number].at[index] if index else sources[number]
        rows, half = source.shape
        first = (core if slot == 0 else 1 - core) * half
        target = out_ref.at[
            pl.ds(pl.multiple_of(chip_after(steps) * rows, rows), rows),
            pl.ds(pl.multiple_of(first, half), half),
        ]
        copies.append(pltpu.make_async_copy(source, target, sem.at[len(copies)]))
    for copy in copies:
        copy.start()
    for copy in copies:
        copy.wait()


def place_rows(weights, shape, **rest):
    arrays, picks = weights
    chosen = [(slot, *pick) for slot, part in enumerate(picks) for pick in part]
    return call(
        functools.partial(place_kernel, chosen),
        "place_rows",
        [shape_of(shape)],
        arrays,
        [ANY] * len(arrays),
        scratch=[pltpu.SemaphoreType.DMA((len(chosen),))],
        **rest,
    )[0]


def rows_of(w_ref, first, core, count):
    half = w_ref.shape[0] // 2
    return w_ref[pl.ds(pl.multiple_of(core * half + first, count), count), :]


def out_sum_kernel(*refs):
    inputs, w_ref, out_ref = refs[:-2], refs[-2], refs[-1]
    weight = rows_of(w_ref, 0, core_index(), inputs[0].shape[2])
    first = 0
    for ref in inputs:
        slots, blen, cols = ref.shape
        out_ref[first : first + slots * blen] = dot(ref[...].reshape(slots * blen, cols), weight)
        first += slots * blen


def out_sum(normed, weights, **rest):
    rows = sum(n.shape[0] * n.shape[1] for n in normed)
    return call(
        out_sum_kernel,
        "out_sum",
        [shape_of((rows, weights.shape[1]), F32)],
        [*normed, weights],
        [VMEM] * (len(normed) + 1),
        **rest,
    )[0]


def out_last_kernel(aparts, cap, len_ref, *refs):
    inputs, (w_ref, total_ref, out_ref, held_ref, sem) = refs[:-5], refs[-5:]
    weight = rows_of(w_ref, 0, 1 - core_index(), inputs[0].shape[2])
    lane = lax.axis_index("leaf")
    blen = inputs[0].shape[1]
    row = lax.broadcasted_iota(jnp.int32, (blen, w_ref.shape[1]), 0)
    copies, place = [], 0
    for ref in inputs:
        count = ref.shape[0]
        rows = slice(place * blen, (place + count) * blen)
        total = total_ref[rows] + dot(ref[...].reshape(count * blen, ref.shape[2]), weight)
        for i in range(count):
            slot = (lane ^ aparts[place // cap]) * cap + place % cap
            part = total[i * blen : (i + 1) * blen]
            held_ref[place] = jnp.where(row < len_ref[slot], part, 0.0).astype(BF16)
            copies.append(pltpu.make_async_copy(held_ref.at[place], out_ref.at[slot], sem.at[place]))
            copies[-1].start()
            place += 1
    for copy in copies:
        copy.wait()


def out_last(lengths, normed, aparts, weights, total, **rest):
    slots, blen = lengths.shape[0], normed[0].shape[1]
    shape = (slots, blen, weights.shape[1])
    return call(
        functools.partial(out_last_kernel, aparts, slots // len(aparts)),
        "out_last",
        [shape_of(shape)],
        [lengths, *normed, weights, total],
        [SMEM] + [VMEM] * (2 + len(normed)),
        [ANY],
        scratch=[pltpu.VMEM(shape, BF16), pltpu.SemaphoreType.DMA((slots,))],
        **rest,
    )[0]


def shards(
    trunk_tokens, branch_tokens, fork_offset, fork_tree, branch_len, w_query, w_key, w_value, w_out
):
    lanes, count = lax.axis_size("leaf"), lax.axis_size("trunk")
    bits = [1 << i for i in range(1, count.bit_length() - 1)]
    paired = len(bits) == 2 and lanes % 2 == 0 and (2 * w_key.shape[0]) % DH == 0
    order = []
    chain = functools.partial(touch, order=order)

    if paired:
        kv, qo = [w_key, w_value], [w_query, w_out]
        kv_other = [swap(w, "trunk", 1, "core") for w in kv]
        half = w_key.shape[1] // 2
        kv = [lax.dynamic_slice_in_dim(w, core_index() * half, half, axis=1) for w in kv]
        chain(kv)
        chosen = [(1, [(0, 0, True), (1, 0, True)])]
        (own_kv,) = chip_halves(kv, kv_other, chosen, order=order, weight=40.0)
        near = send_near(own_kv, bits, "kv")
        qo_other = [swap(w, "trunk", 1, "core") for w in qo]
    own_forks = pack_forks(fork_offset, fork_tree, order=order)
    forks = (own_forks, swap(own_forks, "trunk", 1, "forks"))
    trunk_other = swap(trunk_tokens, "trunk", 1, "tokens")
    branch_other = swap(branch_tokens, "trunk", 1, "tokens")
    trunk = trunk_tokens, trunk_other
    if paired:
        chosen = [
            (2, [(0, "even", True)]),
            (2, [(0, "odd", True)]),
            (1, [(1, 0, True), (1, 0, False)]),
            (1, [(1, 0, True), (1, 0, False)]),
        ]
        own_q, other_q, own_o, again_o = chip_halves(qo, qo_other, chosen, order=order, landed=[forks[1]])
        _, near[1] = chain([], through=[near[1]])
        arrays, picks = pair = send_far(near, near[1], bits, "kv")
        at_hand = arrays[:3], [part[:3] for part in picks]
        earlier = trunk_partial(*trunk, at_hand, order=order, landed=[branch_other])
        _, own_q = chain(arrays[3:], through=[own_q])
        near_q = send_near(own_q, bits, "query")
        last = arrays[3:], [[(0, i, steps) for _, i, steps in part[3:]] for part in picks]
    else:
        pair = whole_pair([w_key, w_value], 1, [(0, 0), (1, 0)])
        queries = whole_pair([w_query], 2, [(0, 0), (0, 1)])
        out_full = lax.all_gather(w_out, "trunk", axis=0, tiled=True)
        earlier, last = (), pair

    def scan_round(held, number):
        if paired:
            return [turn(h, 1 + number, bits, "scan") for h in held]
        return [swap(h, "trunk", bits[number]) for h in held]

    mask = bits[1] if paired else 0
    held, first, kept = trunk_states(*trunk, last, mask, 1, earlier, order=order)
    terms = [scan_round(first, 0)]
    if paired:
        _, near_q[1] = chain(near_q[2:], through=[near_q[1]], weight=5.0)
        far_q = turn(near_q[1], 2, bits, "query_far")
        across = [swap(a, "leaf", 1, "query_lane") for a in near_q[1:]]
    for number in range(1, len(bits)):
        held = scan_step(held, terms[-1], bits[0] if paired else 0, order=order)
        terms.append(scan_round(held, number))
    if paired:
        _, far_q = chain([], through=[far_q])
        last_q = swap(far_q, "leaf", 1, "query_lane")
        queries = lane_pieces(near_q, far_q, other_q, [*across, last_q])
    (parts,) = fork_parts(forks, *kept, order=order)
    if paired:
        chain(across, weight=6.0)
    sends = fork_states(
        forks, parts, terms, bits, paired, lanes, order=order, through=[own_o] if paired else []
    )
    far = sorted(range(1, lanes), key=lambda a: a == 1)
    moved = {a: swap(sends[a], "leaf", a, "lane") for a in far}
    received = [sends[0]] + [moved[a] for a in range(1, lanes)]
    if paired:
        held_o = turn(sends[lanes], 1, bits, "out")
        _, again_o = chain([last_q], through=[again_o])
        near_o = [again_o, held_o, turn(again_o, 2, bits, "out")]
    q, intra = branch_parts(
        branch_tokens, branch_other, queries, pair, paired, order=order, weight=20.0
    )
    if paired:
        _, near_o[1] = chain([], through=[held_o])
        outs = send_far(near_o, near_o[1], bits, "out")
    aparts = sorted(range(lanes), key=lambda a: a == 2)
    split = [aparts[:-1], aparts[-1:]] if lanes > 1 else [aparts]
    mine, other = [], []
    for part in split:
        if mine and paired:
            chain(near_o[2:3], weight=1.0)
        own, theirs = norm_parts(q, intra, received, part, order=order, weight=4.0 if mine else 0.5)
        mine.append(own)
        other.append(swap(theirs, "trunk", 1, "normed"))
    if paired:
        chain(other[:1])
        out_full = place_rows(
            outs, (w_out.shape[0] * count, w_out.shape[1]), order=order, weight=8.0
        )
    total = out_sum(mine, out_full, order=order)
    return out_last(branch_len, other, aparts, out_full, total, order=order)


def solution(mesh):
    in_specs = (
        P("leaf", "trunk", None),
        P(("leaf", "trunk"), None, None),
        P("leaf", "trunk", None),
        P("leaf", "trunk", None),
        P(("leaf", "trunk")),
        P("trunk", None),
        P("trunk", None),
        P("trunk", None),
        P("trunk", None),
    )
    out_specs = P(("leaf", "trunk"), None, None)
    return jax.shard_map(shards, mesh=mesh, in_specs=in_specs, out_specs=out_specs, check_vma=False)
```

```python
import functools

import jax
import jax.numpy as jnp
from jax import lax
from jax.experimental import pallas as pl
from jax.experimental.pallas import tpu as pltpu
from jax.sharding import PartitionSpec as P

H = 8
DH = 128
F32 = jnp.float32
BF16 = jnp.bfloat16
VMEM_BYTES = 16 * 1024 * 1024
ANY = pl.BlockSpec(memory_space=pl.ANY)
VMEM = pl.BlockSpec(memory_space=pltpu.VMEM)
SMEM = pl.BlockSpec(memory_space=pltpu.SMEM)


def swap(value, axis, bit, name="rows"):
    with jax.named_scope("to_" + name):
        return lax.ppermute(value, axis, [(i, i ^ bit) for i in range(lax.axis_size(axis))])


def turn(value, step, bits, name):
    bit = lambda i: bits[0] if (i % 2 == 0) == (step == 1) else bits[1]
    with jax.named_scope("to_" + name):
        count = lax.axis_size("trunk")
        return lax.ppermute(value, "trunk", [(i, i ^ bit(i)) for i in range(count)])


def dot(left, right):
    return jnp.dot(left, right, preferred_element_type=F32)


def shape_of(shape, dtype=BF16):
    return jax.ShapeDtypeStruct(tuple(shape), dtype)


def call(kernel, name, outs, inputs, specs, out_specs=None, scratch=(), order=None, through=(), landed=(), weight=0.0):
    after = (*(order or ()), *landed)
    n, t, w, m = len(inputs), len(through), len(after), len(outs)

    def body(*refs):
        kernel(*refs[:n], *refs[n + t + w : n + t + w + m], *refs[n + 2 * t + w + m :])

    results = pl.pallas_call(
        body,
        out_shape=[*outs, *(shape_of(a.shape, a.dtype) for a in through)],
        in_specs=[*specs, *[ANY] * (t + w)],
        out_specs=[*(out_specs or [VMEM] * m), *[ANY] * t],
        scratch_shapes=list(scratch),
        input_output_aliases={n + i: m + i for i in range(t)},
        compiler_params=pltpu.CompilerParams(vmem_limit_bytes=VMEM_BYTES),
        cost_estimate=pl.CostEstimate(
            flops=int(weight * 1e9), bytes_accessed=0, transcendentals=0
        ),
        name=name,
    )(*inputs, *through, *after)
    if order is not None:
        order[:] = [results[0]]
    return results


def core_index():
    return lax.axis_index("trunk") % 2


def chip_index():
    return lax.axis_index("trunk") // 2


def touch_kernel(*refs):
    refs[-1][...] = jnp.zeros_like(refs[-1])


def touch(arrays, **rest):
    return call(touch_kernel, "touch", [shape_of((8, DH), F32)], arrays, [ANY] * len(arrays), **rest)


def halves_kernel(count, chosen, *refs):
    core, odd = core_index(), lax.axis_index("leaf") % 2
    mine, other, outs, sem = refs[:count], refs[count : 2 * count], refs[2 * count : -1], refs[-1]
    copies = []
    for out, (parts, picks) in zip(outs, chosen):
        for slot, (i, p, own) in enumerate(picks):
            rows, width = other[i].shape
            part = width // 2 // parts
            p = {"even": odd, "odd": 1 - odd}.get(p, p)
            first = (core if own else 1 - core) * (width // 2) + p * part
            columns = pl.ds(pl.multiple_of(first, part), part)
            for source, place in ((mine[i], core), (other[i], 1 - core)):
                target = out.at[slot, pl.ds(pl.multiple_of(place * rows, rows), rows)]
                part_of = source if source.shape[1] == part else source.at[:, columns]
                copies.append(pltpu.make_async_copy(part_of, target, sem.at[len(copies)]))
    for copy in copies:
        copy.start()
    for copy in copies:
        copy.wait()


def chip_halves(mine, other, chosen, **rest):
    rows, width = other[0].shape
    return call(
        functools.partial(halves_kernel, len(mine), chosen),
        "chip_halves",
        [shape_of((len(picks), 2 * rows, width // 2 // parts)) for parts, picks in chosen],
        [*mine, *other],
        [ANY] * (2 * len(mine)),
        scratch=[pltpu.SemaphoreType.DMA((sum(2 * len(picks) for _, picks in chosen),))],
        **rest,
    )


def send_near(pair, bits, name):
    return [pair, *(turn(pair, step, bits, name) for step in (1, 2))]


def send_far(near, held, bits, name):
    arrays = [*near, turn(held, 2, bits, name + "_far")]
    return arrays, [[(i, (slot,), i) for i in range(4)] for slot in range(near[0].shape[0])]


def lane_pieces(near, far, other, across):
    arrays = [*near, far, other, *across]
    return arrays, [[(4 * i + k, (0,), k) for k in range(4)] for i in range(2)]


def whole_pair(weights, parts, chosen):
    arrays = []
    for i, p in chosen:
        full = lax.all_gather(weights[i], "trunk", axis=0, tiled=True)
        part = full.shape[1] // 2 // parts
        start = core_index() * (full.shape[1] // 2) + p * part
        arrays.append(lax.dynamic_slice_in_dim(full, start, part, axis=1))
    return arrays, [[(i, (), None)] for i in range(len(arrays))]


def chip_after(steps):
    first = jnp.where(core_index() == 0, 1, 2)
    return chip_index() ^ (0, first, 3 - first, 3)[steps]


def project(x_ref, lead, picks, refs):
    total = None
    for number, index, steps in picks:
        weight = refs[number][index] if index else refs[number][...]
        depth = weight.shape[0]
        if steps is None:
            left = x_ref[lead]
        else:
            left = x_ref[lead, :, pl.ds(pl.multiple_of(chip_after(steps) * depth, depth), depth)]
        term = dot(left, weight)
        total = term if total is None else total + term
    return total


def pack_kernel(offset_ref, tree_ref, out_ref):
    out_ref[0:1] = offset_ref[0]
    out_ref[1:2] = tree_ref[0]


def pack_forks(offset, tree, **rest):
    return call(
        pack_kernel,
        "pack_forks",
        [shape_of((2, offset.shape[2]), jnp.int32)],
        [offset, tree],
        [VMEM] * 2,
        **rest,
    )[0]


def partial_kernel(picks, *refs):
    xs, weights, outs = refs[:2], refs[2:-2], refs[-2:]
    for side in range(2):
        for tree in range(xs[0].shape[0]):
            for part, out in zip(picks, outs):
                out[side, tree] = project(xs[side], tree, part, weights)


def trunk_partial(mine, other, weights, **rest):
    trees, tok, _ = mine.shape
    arrays, picks = weights
    return call(
        functools.partial(partial_kernel, picks),
        "trunk_partial",
        [shape_of((2, trees, tok, arrays[0].shape[-1]), F32)] * 2,
        [mine, other, *arrays],
        [VMEM] * (2 + len(arrays)),
        **rest,
    )


def trunk_kernel(picks, mask, count, parts, *refs):
    xs, earlier, weights = refs[:2], refs[2 : 2 + count], refs[2 + count : -3 - 2 * parts]
    totals, firsts = refs[-3 - 2 * parts : -3 - parts], refs[-3 - parts : -3]
    keys_ref, values_ref, state_ref = refs[-3:]
    sent = (core_index() == 0) | ((lax.axis_index("trunk") & mask) == 0)
    trees, heads = state_ref.shape[1:3]
    for side in range(2):
        for tree in range(trees):
            keys, values = (project(xs[side], tree, part, weights) for part in picks)
            if earlier:
                keys, values = keys + earlier[0][side, tree], values + earlier[1][side, tree]
            keys, values = keys.astype(BF16), values.astype(BF16)
            keys_ref[side, tree] = keys
            values_ref[side, tree] = values
            for h in range(heads):
                at = slice(h * DH, (h + 1) * DH)
                state = lax.dot_general(
                    keys[:, at], values[:, at], (((0,), (0,)), ((), ())), preferred_element_type=F32
                )
                state_ref[side, tree, h] = state
                if side:
                    total = (state_ref[0, tree, h] + state).astype(BF16)
                    part, place = divmod(h, heads // parts)
                    totals[part][tree, place] = total
                    firsts[part][tree, place] = jnp.where(sent, total, jnp.zeros_like(total))


def trunk_states(mine, other, weights, mask, parts, earlier=(), **rest):
    trees, tok, width = mine.shape
    arrays, picks = weights
    cols = arrays[0].shape[-1]
    heads = cols // DH
    parts = parts if heads % parts == 0 else 1
    out = call(
        functools.partial(trunk_kernel, picks, mask, len(earlier), parts),
        "trunk_states",
        [
            *[shape_of((trees, heads // parts, DH, DH))] * (2 * parts),
            shape_of((2, trees, tok, cols)),
            shape_of((2, trees, tok, cols)),
            shape_of((2, trees, heads, DH, DH), F32),
        ],
        [mine, other, *earlier, *arrays],
        [VMEM] * (2 + len(earlier) + len(arrays)),
        **rest,
    )
    return out[:parts], out[parts : 2 * parts], out[2 * parts :]


def part_kernel(mine_ref, other_ref, keys_ref, values_ref, state_ref, fork_ref):
    core = core_index()
    tok = keys_ref.shape[2]
    entries, heads = fork_ref.shape[1:3]
    place = lax.broadcasted_iota(jnp.int32, (tok, DH), 0)
    for side in range(2):
        ints = other_ref if side else mine_ref
        for e in range(entries):
            tree = ints[1, e]
            inside = place < ints[0, e]
            odd = core != side
            for h in range(heads):
                at = slice(h * DH, (h + 1) * DH)
                keys = keys_ref[side, tree, :, at]
                part = lax.dot_general(
                    jnp.where(inside, keys, jnp.zeros_like(keys)),
                    values_ref[side, tree, :, at],
                    (((0,), (0,)), ((), ())),
                    preferred_element_type=F32,
                )
                lower = state_ref[1 - side, tree, h]
                fork_ref[side, e, h] = part + jnp.where(odd, lower, jnp.zeros_like(lower))


def fork_parts(forks, keys, values, states, **rest):
    _, _, tok, cols = keys.shape
    entries, heads = forks[0].shape[1], cols // DH
    return call(
        part_kernel,
        "fork_parts",
        [shape_of((2, entries, heads, DH, DH), F32)],
        [*forks, keys, values, states],
        [SMEM] * 2 + [VMEM] * 3,
        **rest,
    )


def scan_kernel(mask, count, *refs):
    adds = (core_index() == 0) | ((lax.axis_index("trunk") & mask) == 0)
    for held_ref, in_ref, out_ref in zip(refs[:count], refs[count : 2 * count], refs[2 * count :]):
        held = held_ref[...].astype(F32)
        if mask:
            held = jnp.where(adds, held, jnp.zeros_like(held))
        out_ref[...] = (held + in_ref[...].astype(F32)).astype(BF16)


def scan_step(held, received, mask, **rest):
    return call(
        functools.partial(scan_kernel, mask, len(held)),
        "scan_step",
        [shape_of(h.shape) for h in held],
        [*held, *received],
        [VMEM] * (2 * len(held)),
        **rest,
    )


def fork_kernel(masks, both, lanes, parts, *refs):
    count = len(masks) * parts
    ints, fork_ref, terms = refs[:2], refs[2], refs[3 : 3 + count]
    outs, carried_ref = refs[-1 - lanes : -1], refs[-1]
    index, lane = lax.axis_index("trunk"), lax.axis_index("leaf")
    cap = outs[0].shape[1]
    heads = terms[0].shape[1]
    for part in range(parts):
        carried = None
        for mask, ref in zip(masks, terms[part::parts]):
            term = ref[...].astype(F32)
            counts = (index & mask) != 0
            if both:
                counts = counts | (core_index() == 1)
            term = jnp.where(counts, term, jnp.zeros_like(term))
            carried = term if carried is None else carried + term
        carried_ref[:, part * heads : (part + 1) * heads] = carried
    for apart in range(lanes):
        for side in range(2):
            for c in range(cap):
                entry = (lane ^ apart) * cap + c
                state = fork_ref[side, entry] + carried_ref[ints[side][1, entry]]
                outs[apart][side, c] = state.astype(BF16)


def fork_states(forks, parts, terms, masks, both, lanes, **rest):
    _, entries, heads = parts.shape[:3]
    shape = (2, entries // lanes, heads, DH, DH)
    return call(
        functools.partial(fork_kernel, masks, both, lanes, len(terms[0])),
        "fork_states",
        [shape_of(shape)] * lanes,
        [*forks, parts, *(t for term in terms for t in term)],
        [SMEM] * 2 + [VMEM] * (1 + len(terms) * len(terms[0])),
        scratch=[pltpu.VMEM((terms[0][0].shape[0], heads, DH, DH), F32)],
        **rest,
    )


def branch_kernel(counts, picks, by_lane, blen, *refs):
    odd = lax.axis_index("leaf") % 2
    xs, q_out, intra_out = refs[:2], *refs[-2:]
    query_refs, weights = refs[2 : 2 + counts[0]], refs[2 + counts[0] : -2]
    rows = xs[0].shape[1]
    row = lax.broadcasted_iota(jnp.int32, (rows, rows), 0)
    column = lax.broadcasted_iota(jnp.int32, (rows, rows), 1)
    seen = (column <= row) & (column >= row - lax.rem(row, blen))
    for side in range(2):
        for slot in range(xs[0].shape[0]):
            for i, part in enumerate(picks[0]):
                q = project(xs[side], slot, part, query_refs).astype(BF16)
                place = (odd if i == 0 else 1 - odd) if by_lane else i
                first = pl.multiple_of(place * q.shape[1], q.shape[1])
                q_out[side, slot, :, pl.ds(first, q.shape[1])] = q
            k, v = (project(xs[side], slot, part, weights).astype(BF16) for part in picks[1])
            for h in range(k.shape[1] // DH):
                at = slice(h * DH, (h + 1) * DH)
                scores = lax.dot_general(
                    q_out[side, slot, :, at],
                    k[:, at],
                    (((1,), (1,)), ((), ())),
                    preferred_element_type=F32,
                )
                scores = jnp.where(seen, scores, 0.0).astype(BF16)
                intra_out[side, slot, :, at] = dot(scores, v[:, at])


def branch_parts(mine, other, queries, pair, by_lane, **rest):
    slots, blen, width = mine.shape
    join = 2 if slots % 2 == 0 else 1
    mine, other = (a.reshape(slots // join, join * blen, width) for a in (mine, other))
    weights = [queries, pair]
    arrays = [a for held, _ in weights for a in held]
    cols = pair[0][0].shape[-1]
    lead = (2, slots // join, join * blen, cols)
    outs = call(
        functools.partial(
            branch_kernel, [len(held) for held, _ in weights], [p for _, p in weights], by_lane, blen
        ),
        "branch_parts",
        [shape_of(lead), shape_of(lead, F32)],
        [mine, other, *arrays],
        [VMEM] * (2 + len(arrays)),
        **rest,
    )
    return [o.reshape(2, slots, blen, cols) for o in outs]


def norm_kernel(aparts, q_ref, intra_ref, *refs):
    states, outs = refs[: len(aparts)], refs[len(aparts) :]
    lane = lax.axis_index("leaf")
    cap, heads = states[0].shape[1:3]
    for number, apart in enumerate(aparts):
        for side in range(2):
            for c in range(cap):
                slot = (lane ^ apart) * cap + c
                for h in range(heads):
                    at = slice(h * DH, (h + 1) * DH)
                    total = intra_ref[side, slot, :, at] + dot(
                        q_ref[side, slot, :, at], states[number][side, c, h]
                    )
                    meansq = jnp.mean(total * total, axis=-1, keepdims=True)
                    normed = (total * lax.rsqrt(meansq + 1e-06)).astype(BF16)
                    outs[side][number * cap + c, :, at] = normed


def norm_parts(queries, intra, states, aparts, **rest):
    _, _, blen, cols = queries.shape
    count = len(aparts) * states[0].shape[1]
    return call(
        functools.partial(norm_kernel, aparts),
        "norm_parts",
        [shape_of((count, blen, cols))] * 2,
        [queries, intra, *(states[a] for a in aparts)],
        [VMEM] * (2 + len(aparts)),
        **rest,
    )


def place_kernel(picks, *refs):
    core = core_index()
    sources, out_ref, sem = refs[:-2], refs[-2], refs[-1]
    copies = []
    for slot, number, index, steps in picks:
        source = sources[number].at[index] if index else sources[number]
        rows, half = source.shape
        first = (core if slot == 0 else 1 - core) * half
        target = out_ref.at[
            pl.ds(pl.multiple_of(chip_after(steps) * rows, rows), rows),
            pl.ds(pl.multiple_of(first, half), half),
        ]
        copies.append(pltpu.make_async_copy(source, target, sem.at[len(copies)]))
    for copy in copies:
        copy.start()
    for copy in copies:
        copy.wait()


def place_rows(weights, shape, **rest):
    arrays, picks = weights
    chosen = [(slot, *pick) for slot, part in enumerate(picks) for pick in part]
    return call(
        functools.partial(place_kernel, chosen),
        "place_rows",
        [shape_of(shape)],
        arrays,
        [ANY] * len(arrays),
        scratch=[pltpu.SemaphoreType.DMA((len(chosen),))],
        **rest,
    )[0]


def rows_of(w_ref, first, core, count):
    half = w_ref.shape[0] // 2
    return w_ref[pl.ds(pl.multiple_of(core * half + first, count), count), :]


def out_sum_kernel(*refs):
    inputs, w_ref, out_ref = refs[:-2], refs[-2], refs[-1]
    weight = rows_of(w_ref, 0, core_index(), inputs[0].shape[2])
    first = 0
    for ref in inputs:
        slots, blen, cols = ref.shape
        out_ref[first : first + slots * blen] = dot(ref[...].reshape(slots * blen, cols), weight)
        first += slots * blen


def out_sum(normed, weights, **rest):
    rows = sum(n.shape[0] * n.shape[1] for n in normed)
    return call(
        out_sum_kernel,
        "out_sum",
        [shape_of((rows, weights.shape[1]), F32)],
        [*normed, weights],
        [VMEM] * (len(normed) + 1),
        **rest,
    )[0]


def out_last_kernel(aparts, cap, len_ref, *refs):
    inputs, (w_ref, total_ref, out_ref, held_ref, sem) = refs[:-5], refs[-5:]
    weight = rows_of(w_ref, 0, 1 - core_index(), inputs[0].shape[2])
    lane = lax.axis_index("leaf")
    blen = inputs[0].shape[1]
    row = lax.broadcasted_iota(jnp.int32, (blen, w_ref.shape[1]), 0)
    copies, place = [], 0
    for ref in inputs:
        count = ref.shape[0]
        rows = slice(place * blen, (place + count) * blen)
        total = total_ref[rows] + dot(ref[...].reshape(count * blen, ref.shape[2]), weight)
        for i in range(count):
            slot = (lane ^ aparts[place // cap]) * cap + place % cap
            part = total[i * blen : (i + 1) * blen]
            held_ref[place] = jnp.where(row < len_ref[slot], part, 0.0).astype(BF16)
            copies.append(pltpu.make_async_copy(held_ref.at[place], out_ref.at[slot], sem.at[place]))
            copies[-1].start()
            place += 1
    for copy in copies:
        copy.wait()


def out_last(lengths, normed, aparts, weights, total, **rest):
    slots, blen = lengths.shape[0], normed[0].shape[1]
    shape = (slots, blen, weights.shape[1])
    return call(
        functools.partial(out_last_kernel, aparts, slots // len(aparts)),
        "out_last",
        [shape_of(shape)],
        [lengths, *normed, weights, total],
        [SMEM] + [VMEM] * (2 + len(normed)),
        [ANY],
        scratch=[pltpu.VMEM(shape, BF16), pltpu.SemaphoreType.DMA((slots,))],
        **rest,
    )[0]


def shards(
    trunk_tokens, branch_tokens, fork_offset, fork_tree, branch_len, w_query, w_key, w_value, w_out
):
    lanes, count = lax.axis_size("leaf"), lax.axis_size("trunk")
    bits = [1 << i for i in range(1, count.bit_length() - 1)]
    paired = len(bits) == 2 and lanes % 2 == 0 and (2 * w_key.shape[0]) % DH == 0
    order = []
    chain = functools.partial(touch, order=order)

    if paired:
        kv, qo = [w_key, w_value], [w_query, w_out]
        kv_other = [swap(w, "trunk", 1, "core") for w in kv]
        half = w_key.shape[1] // 2
        kv = [lax.dynamic_slice_in_dim(w, core_index() * half, half, axis=1) for w in kv]
        chain(kv)
        chosen = [(1, [(0, 0, True), (1, 0, True)])]
        (own_kv,) = chip_halves(kv, kv_other, chosen, order=order, weight=40.0)
        near = send_near(own_kv, bits, "kv")
        qo_other = [swap(w, "trunk", 1, "core") for w in qo]
    own_forks = pack_forks(fork_offset, fork_tree, order=order)
    forks = (own_forks, swap(own_forks, "trunk", 1, "forks"))
    trunk_other = swap(trunk_tokens, "trunk", 1, "tokens")
    branch_other = swap(branch_tokens, "trunk", 1, "tokens")
    trunk = trunk_tokens, trunk_other
    if paired:
        chosen = [
            (2, [(0, "even", True)]),
            (2, [(0, "odd", True)]),
            (1, [(1, 0, True), (1, 0, False)]),
            (1, [(1, 0, True), (1, 0, False)]),
        ]
        own_q, other_q, own_o, again_o = chip_halves(qo, qo_other, chosen, order=order, landed=[forks[1]])
        _, near[1] = chain([], through=[near[1]])
        arrays, picks = pair = send_far(near, near[1], bits, "kv")
        at_hand = arrays[:3], [part[:3] for part in picks]
        earlier = trunk_partial(*trunk, at_hand, order=order, landed=[branch_other])
        _, own_q = chain(arrays[3:], through=[own_q])
        near_q = send_near(own_q, bits, "query")
        last = arrays[3:], [[(0, i, steps) for _, i, steps in part[3:]] for part in picks]
    else:
        pair = whole_pair([w_key, w_value], 1, [(0, 0), (1, 0)])
        queries = whole_pair([w_query], 2, [(0, 0), (0, 1)])
        out_full = lax.all_gather(w_out, "trunk", axis=0, tiled=True)
        earlier, last = (), pair

    def scan_round(held, number):
        if paired:
            return [turn(h, 1 + number, bits, "scan") for h in held]
        return [swap(h, "trunk", bits[number]) for h in held]

    mask = bits[1] if paired else 0
    held, first, kept = trunk_states(*trunk, last, mask, 1, earlier, order=order)
    terms = [scan_round(first, 0)]
    if paired:
        _, near_q[1] = chain(near_q[2:], through=[near_q[1]], weight=5.0)
        far_q = turn(near_q[1], 2, bits, "query_far")
        across = [swap(a, "leaf", 1, "query_lane") for a in near_q[1:]]
    for number in range(1, len(bits)):
        held = scan_step(held, terms[-1], bits[0] if paired else 0, order=order)
        terms.append(scan_round(held, number))
    if paired:
        _, far_q = chain([], through=[far_q])
        last_q = swap(far_q, "leaf", 1, "query_lane")
        queries = lane_pieces(near_q, far_q, other_q, [*across, last_q])
    (parts,) = fork_parts(forks, *kept, order=order)
    if paired:
        chain(across, weight=6.0)
    sends = fork_states(
        forks, parts, terms, bits, paired, lanes, order=order, through=[own_o] if paired else []
    )
    far = sorted(range(1, lanes), key=lambda a: a == 1)
    moved = {a: swap(sends[a], "leaf", a, "lane") for a in far}
    received = [sends[0]] + [moved[a] for a in range(1, lanes)]
    if paired:
        held_o = turn(sends[lanes], 1, bits, "out")
        _, again_o = chain([last_q], through=[again_o])
        near_o = [again_o, held_o, turn(again_o, 2, bits, "out")]
    q, intra = branch_parts(
        branch_tokens, branch_other, queries, pair, paired, order=order, weight=20.0
    )
    if paired:
        _, near_o[1] = chain([], through=[held_o])
        outs = send_far(near_o, near_o[1], bits, "out")
    aparts = sorted(range(lanes), key=lambda a: a == 2)
    split = [aparts[:-1], aparts[-1:]] if lanes > 1 else [aparts]
    mine, other = [], []
    for part in split:
        if mine and paired:
            chain(near_o[2:3], weight=1.0)
        own, theirs = norm_parts(q, intra, received, part, order=order, weight=4.0 if mine else 0.5)
        mine.append(own)
        other.append(swap(theirs, "trunk", 1, "normed"))
    if paired:
        chain(other[:1])
        out_full = place_rows(
            outs, (w_out.shape[0] * count, w_out.shape[1]), order=order, weight=8.0
        )
    total = out_sum(mine, out_full, order=order)
    return out_last(branch_len, other, aparts, out_full, total, order=order)


def solution(mesh):
    in_specs = (
        P("leaf", "trunk", None),
        P(("leaf", "trunk"), None, None),
        P("leaf", "trunk", None),
        P("leaf", "trunk", None),
        P(("leaf", "trunk")),
        P("trunk", None),
        P("trunk", None),
        P("trunk", None),
        P("trunk", None),
    )
    out_specs = P(("leaf", "trunk"), None, None)
    return jax.shard_map(shards, mesh=mesh, in_specs=in_specs, out_specs=out_specs, check_vma=False)
```

```python
import functools

import jax
import jax.numpy as jnp
from jax import lax
from jax.experimental import pallas as pl
from jax.experimental.pallas import tpu as pltpu
from jax.sharding import PartitionSpec as P

H = 8
DH = 128
F32 = jnp.float32
BF16 = jnp.bfloat16
VMEM_BYTES = 16 * 1024 * 1024
ANY = pl.BlockSpec(memory_space=pl.ANY)
VMEM = pl.BlockSpec(memory_space=pltpu.VMEM)
SMEM = pl.BlockSpec(memory_space=pltpu.SMEM)


def swap(value, axis, bit, name="rows"):
    with jax.named_scope("to_" + name):
        return lax.ppermute(value, axis, [(i, i ^ bit) for i in range(lax.axis_size(axis))])


def turn(value, step, bits, name):
    bit = lambda i: bits[0] if (i % 2 == 0) == (step == 1) else bits[1]
    with jax.named_scope("to_" + name):
        count = lax.axis_size("trunk")
        return lax.ppermute(value, "trunk", [(i, i ^ bit(i)) for i in range(count)])


def dot(left, right):
    return jnp.dot(left, right, preferred_element_type=F32)


def shape_of(shape, dtype=BF16):
    return jax.ShapeDtypeStruct(tuple(shape), dtype)


def call(kernel, name, outs, inputs, specs, out_specs=None, scratch=(), order=None, through=(), landed=(), weight=0.0):
    after = (*(order or ()), *landed)
    n, t, w, m = len(inputs), len(through), len(after), len(outs)

    def body(*refs):
        kernel(*refs[:n], *refs[n + t + w : n + t + w + m], *refs[n + 2 * t + w + m :])

    results = pl.pallas_call(
        body,
        out_shape=[*outs, *(shape_of(a.shape, a.dtype) for a in through)],
        in_specs=[*specs, *[ANY] * (t + w)],
        out_specs=[*(out_specs or [VMEM] * m), *[ANY] * t],
        scratch_shapes=list(scratch),
        input_output_aliases={n + i: m + i for i in range(t)},
        compiler_params=pltpu.CompilerParams(vmem_limit_bytes=VMEM_BYTES),
        cost_estimate=pl.CostEstimate(
            flops=int(weight * 1e9), bytes_accessed=0, transcendentals=0
        ),
        name=name,
    )(*inputs, *through, *after)
    if order is not None:
        order[:] = [results[0]]
    return results


def core_index():
    return lax.axis_index("trunk") % 2


def chip_index():
    return lax.axis_index("trunk") // 2


def touch_kernel(*refs):
    refs[-1][...] = jnp.zeros_like(refs[-1])


def touch(arrays, **rest):
    return call(touch_kernel, "touch", [shape_of((8, DH), F32)], arrays, [ANY] * len(arrays), **rest)


def halves_kernel(count, chosen, *refs):
    core, odd = core_index(), lax.axis_index("leaf") % 2
    mine, other, outs, sem = refs[:count], refs[count : 2 * count], refs[2 * count : -1], refs[-1]
    copies = []
    for out, (parts, picks) in zip(outs, chosen):
        for slot, (i, p, own) in enumerate(picks):
            rows, width = other[i].shape
            part = width // 2 // parts
            p = {"even": odd, "odd": 1 - odd}.get(p, p)
            first = (core if own else 1 - core) * (width // 2) + p * part
            columns = pl.ds(pl.multiple_of(first, part), part)
            for source, place in ((mine[i], core), (other[i], 1 - core)):
                target = out.at[slot, pl.ds(pl.multiple_of(place * rows, rows), rows)]
                part_of = source if source.shape[1] == part else source.at[:, columns]
                copies.append(pltpu.make_async_copy(part_of, target, sem.at[len(copies)]))
    for copy in copies:
        copy.start()
    for copy in copies:
        copy.wait()


def chip_halves(mine, other, chosen, **rest):
    rows, width = other[0].shape
    return call(
        functools.partial(halves_kernel, len(mine), chosen),
        "chip_halves",
        [shape_of((len(picks), 2 * rows, width // 2 // parts)) for parts, picks in chosen],
        [*mine, *other],
        [ANY] * (2 * len(mine)),
        scratch=[pltpu.SemaphoreType.DMA((sum(2 * len(picks) for _, picks in chosen),))],
        **rest,
    )


def send_near(pair, bits, name):
    return [pair, *(turn(pair, step, bits, name) for step in (1, 2))]


def send_far(near, held, bits, name):
    arrays = [*near, turn(held, 2, bits, name + "_far")]
    return arrays, [[(i, (slot,), i) for i in range(4)] for slot in range(near[0].shape[0])]


def lane_pieces(near, far, other, across):
    arrays = [*near, far, other, *across]
    return arrays, [[(4 * i + k, (0,), k) for k in range(4)] for i in range(2)]


def whole_pair(weights, parts, chosen):
    arrays = []
    for i, p in chosen:
        full = lax.all_gather(weights[i], "trunk", axis=0, tiled=True)
        part = full.shape[1] // 2 // parts
        start = core_index() * (full.shape[1] // 2) + p * part
        arrays.append(lax.dynamic_slice_in_dim(full, start, part, axis=1))
    return arrays, [[(i, (), None)] for i in range(len(arrays))]


def chip_after(steps):
    first = jnp.where(core_index() == 0, 1, 2)
    return chip_index() ^ (0, first, 3 - first, 3)[steps]


def project(x_ref, lead, picks, refs):
    total = None
    for number, index, steps in picks:
        weight = refs[number][index] if index else refs[number][...]
        depth = weight.shape[0]
        if steps is None:
            left = x_ref[lead]
        else:
            left = x_ref[lead, :, pl.ds(pl.multiple_of(chip_after(steps) * depth, depth), depth)]
        term = dot(left, weight)
        total = term if total is None else total + term
    return total


def pack_kernel(offset_ref, tree_ref, out_ref):
    out_ref[0:1] = offset_ref[0]
    out_ref[1:2] = tree_ref[0]


def pack_forks(offset, tree, **rest):
    return call(
        pack_kernel,
        "pack_forks",
        [shape_of((2, offset.shape[2]), jnp.int32)],
        [offset, tree],
        [VMEM] * 2,
        **rest,
    )[0]


def partial_kernel(picks, *refs):
    xs, weights, outs = refs[:2], refs[2:-2], refs[-2:]
    for side in range(2):
        for tree in range(xs[0].shape[0]):
            for part, out in zip(picks, outs):
                out[side, tree] = project(xs[side], tree, part, weights)


def trunk_partial(mine, other, weights, **rest):
    trees, tok, _ = mine.shape
    arrays, picks = weights
    return call(
        functools.partial(partial_kernel, picks),
        "trunk_partial",
        [shape_of((2, trees, tok, arrays[0].shape[-1]), F32)] * 2,
        [mine, other, *arrays],
        [VMEM] * (2 + len(arrays)),
        **rest,
    )


def trunk_kernel(picks, mask, count, parts, *refs):
    xs, earlier, weights = refs[:2], refs[2 : 2 + count], refs[2 + count : -3 - 2 * parts]
    totals, firsts = refs[-3 - 2 * parts : -3 - parts], refs[-3 - parts : -3]
    keys_ref, values_ref, state_ref = refs[-3:]
    sent = (core_index() == 0) | ((lax.axis_index("trunk") & mask) == 0)
    trees, heads = state_ref.shape[1:3]
    for side in range(2):
        for tree in range(trees):
            keys, values = (project(xs[side], tree, part, weights) for part in picks)
            if earlier:
                keys, values = keys + earlier[0][side, tree], values + earlier[1][side, tree]
            keys, values = keys.astype(BF16), values.astype(BF16)
            keys_ref[side, tree] = keys
            values_ref[side, tree] = values
            for h in range(heads):
                at = slice(h * DH, (h + 1) * DH)
                state = lax.dot_general(
                    keys[:, at], values[:, at], (((0,), (0,)), ((), ())), preferred_element_type=F32
                )
                state_ref[side, tree, h] = state
                if side:
                    total = (state_ref[0, tree, h] + state).astype(BF16)
                    part, place = divmod(h, heads // parts)
                    totals[part][tree, place] = total
                    firsts[part][tree, place] = jnp.where(sent, total, jnp.zeros_like(total))


def trunk_states(mine, other, weights, mask, parts, earlier=(), **rest):
    trees, tok, width = mine.shape
    arrays, picks = weights
    cols = arrays[0].shape[-1]
    heads = cols // DH
    parts = parts if heads % parts == 0 else 1
    out = call(
        functools.partial(trunk_kernel, picks, mask, len(earlier), parts),
        "trunk_states",
        [
            *[shape_of((trees, heads // parts, DH, DH))] * (2 * parts),
            shape_of((2, trees, tok, cols)),
            shape_of((2, trees, tok, cols)),
            shape_of((2, trees, heads, DH, DH), F32),
        ],
        [mine, other, *earlier, *arrays],
        [VMEM] * (2 + len(earlier) + len(arrays)),
        **rest,
    )
    return out[:parts], out[parts : 2 * parts], out[2 * parts :]


def part_kernel(mine_ref, other_ref, keys_ref, values_ref, state_ref, fork_ref):
    core = core_index()
    tok = keys_ref.shape[2]
    entries, heads = fork_ref.shape[1:3]
    place = lax.broadcasted_iota(jnp.int32, (tok, DH), 0)
    for side in range(2):
        ints = other_ref if side else mine_ref
        for e in range(entries):
            tree = ints[1, e]
            inside = place < ints[0, e]
            odd = core != side
            for h in range(heads):
                at = slice(h * DH, (h + 1) * DH)
                keys = keys_ref[side, tree, :, at]
                part = lax.dot_general(
                    jnp.where(inside, keys, jnp.zeros_like(keys)),
                    values_ref[side, tree, :, at],
                    (((0,), (0,)), ((), ())),
                    preferred_element_type=F32,
                )
                lower = state_ref[1 - side, tree, h]
                fork_ref[side, e, h] = part + jnp.where(odd, lower, jnp.zeros_like(lower))


def fork_parts(forks, keys, values, states, **rest):
    _, _, tok, cols = keys.shape
    entries, heads = forks[0].shape[1], cols // DH
    return call(
        part_kernel,
        "fork_parts",
        [shape_of((2, entries, heads, DH, DH), F32)],
        [*forks, keys, values, states],
        [SMEM] * 2 + [VMEM] * 3,
        **rest,
    )


def scan_kernel(mask, count, *refs):
    adds = (core_index() == 0) | ((lax.axis_index("trunk") & mask) == 0)
    for held_ref, in_ref, out_ref in zip(refs[:count], refs[count : 2 * count], refs[2 * count :]):
        held = held_ref[...].astype(F32)
        if mask:
            held = jnp.where(adds, held, jnp.zeros_like(held))
        out_ref[...] = (held + in_ref[...].astype(F32)).astype(BF16)


def scan_step(held, received, mask, **rest):
    return call(
        functools.partial(scan_kernel, mask, len(held)),
        "scan_step",
        [shape_of(h.shape) for h in held],
        [*held, *received],
        [VMEM] * (2 * len(held)),
        **rest,
    )


def fork_kernel(masks, both, lanes, parts, *refs):
    count = len(masks) * parts
    ints, fork_ref, terms = refs[:2], refs[2], refs[3 : 3 + count]
    outs, carried_ref = refs[-1 - lanes : -1], refs[-1]
    index, lane = lax.axis_index("trunk"), lax.axis_index("leaf")
    cap = outs[0].shape[1]
    heads = terms[0].shape[1]
    for part in range(parts):
        carried = None
        for mask, ref in zip(masks, terms[part::parts]):
            term = ref[...].astype(F32)
            counts = (index & mask) != 0
            if both:
                counts = counts | (core_index() == 1)
            term = jnp.where(counts, term, jnp.zeros_like(term))
            carried = term if carried is None else carried + term
        carried_ref[:, part * heads : (part + 1) * heads] = carried
    for apart in range(lanes):
        for side in range(2):
            for c in range(cap):
                entry = (lane ^ apart) * cap + c
                state = fork_ref[side, entry] + carried_ref[ints[side][1, entry]]
                outs[apart][side, c] = state.astype(BF16)


def fork_states(forks, parts, terms, masks, both, lanes, **rest):
    _, entries, heads = parts.shape[:3]
    shape = (2, entries // lanes, heads, DH, DH)
    return call(
        functools.partial(fork_kernel, masks, both, lanes, len(terms[0])),
        "fork_states",
        [shape_of(shape)] * lanes,
        [*forks, parts, *(t for term in terms for t in term)],
        [SMEM] * 2 + [VMEM] * (1 + len(terms) * len(terms[0])),
        scratch=[pltpu.VMEM((terms[0][0].shape[0], heads, DH, DH), F32)],
        **rest,
    )


def branch_kernel(counts, picks, by_lane, blen, *refs):
    odd = lax.axis_index("leaf") % 2
    xs, q_out, intra_out = refs[:2], *refs[-2:]
    query_refs, weights = refs[2 : 2 + counts[0]], refs[2 + counts[0] : -2]
    rows = xs[0].shape[1]
    row = lax.broadcasted_iota(jnp.int32, (rows, rows), 0)
    column = lax.broadcasted_iota(jnp.int32, (rows, rows), 1)
    seen = (column <= row) & (column >= row - lax.rem(row, blen))
    for side in range(2):
        for slot in range(xs[0].shape[0]):
            for i, part in enumerate(picks[0]):
                q = project(xs[side], slot, part, query_refs).astype(BF16)
                place = (odd if i == 0 else 1 - odd) if by_lane else i
                first = pl.multiple_of(place * q.shape[1], q.shape[1])
                q_out[side, slot, :, pl.ds(first, q.shape[1])] = q
            k, v = (project(xs[side], slot, part, weights).astype(BF16) for part in picks[1])
            for h in range(k.shape[1] // DH):
                at = slice(h * DH, (h + 1) * DH)
                scores = lax.dot_general(
                    q_out[side, slot, :, at],
                    k[:, at],
                    (((1,), (1,)), ((), ())),
                    preferred_element_type=F32,
                )
                scores = jnp.where(seen, scores, 0.0).astype(BF16)
                intra_out[side, slot, :, at] = dot(scores, v[:, at])


def branch_parts(mine, other, queries, pair, by_lane, **rest):
    slots, blen, width = mine.shape
    join = 2 if slots % 2 == 0 else 1
    mine, other = (a.reshape(slots // join, join * blen, width) for a in (mine, other))
    weights = [queries, pair]
    arrays = [a for held, _ in weights for a in held]
    cols = pair[0][0].shape[-1]
    lead = (2, slots // join, join * blen, cols)
    outs = call(
        functools.partial(
            branch_kernel, [len(held) for held, _ in weights], [p for _, p in weights], by_lane, blen
        ),
        "branch_parts",
        [shape_of(lead), shape_of(lead, F32)],
        [mine, other, *arrays],
        [VMEM] * (2 + len(arrays)),
        **rest,
    )
    return [o.reshape(2, slots, blen, cols) for o in outs]


def norm_kernel(aparts, q_ref, intra_ref, *refs):
    states, outs = refs[: len(aparts)], refs[len(aparts) :]
    lane = lax.axis_index("leaf")
    cap, heads = states[0].shape[1:3]
    for number, apart in enumerate(aparts):
        for side in range(2):
            for c in range(cap):
                slot = (lane ^ apart) * cap + c
                for h in range(heads):
                    at = slice(h * DH, (h + 1) * DH)
                    total = intra_ref[side, slot, :, at] + dot(
                        q_ref[side, slot, :, at], states[number][side, c, h]
                    )
                    meansq = jnp.mean(total * total, axis=-1, keepdims=True)
                    normed = (total * lax.rsqrt(meansq + 1e-06)).astype(BF16)
                    outs[side][number * cap + c, :, at] = normed


def norm_parts(queries, intra, states, aparts, **rest):
    _, _, blen, cols = queries.shape
    count = len(aparts) * states[0].shape[1]
    return call(
        functools.partial(norm_kernel, aparts),
        "norm_parts",
        [shape_of((count, blen, cols))] * 2,
        [queries, intra, *(states[a] for a in aparts)],
        [VMEM] * (2 + len(aparts)),
        **rest,
    )


def place_kernel(picks, *refs):
    core = core_index()
    sources, out_ref, sem = refs[:-2], refs[-2], refs[-1]
    copies = []
    for slot, number, index, steps, quarter in picks:
        source = sources[number].at[index] if index else sources[number]
        rows, part = source.shape
        first = (core if slot == 0 else 1 - core) * (out_ref.shape[1] // 2) + quarter * part
        target = out_ref.at[
            pl.ds(pl.multiple_of(chip_after(steps) * rows, rows), rows),
            pl.ds(pl.multiple_of(first, part), part),
        ]
        copies.append(pltpu.make_async_copy(source, target, sem.at[len(copies)]))
    for copy in copies:
        copy.start()
    for copy in copies:
        copy.wait()


def place_rows(weights, shape, **rest):
    arrays, picks = weights
    chosen = [(slot, *pick) for slot, part in enumerate(picks) for pick in part]
    return call(
        functools.partial(place_kernel, chosen),
        "place_rows",
        [shape_of(shape)],
        arrays,
        [ANY] * len(arrays),
        scratch=[pltpu.SemaphoreType.DMA((len(chosen),))],
        **rest,
    )[0]


def rows_of(w_ref, first, core, count):
    half = w_ref.shape[0] // 2
    return w_ref[pl.ds(pl.multiple_of(core * half + first, count), count), :]


def out_sum_kernel(*refs):
    inputs, w_ref, out_ref = refs[:-2], refs[-2], refs[-1]
    weight = rows_of(w_ref, 0, core_index(), inputs[0].shape[2])
    first = 0
    for ref in inputs:
        slots, blen, cols = ref.shape
        out_ref[first : first + slots * blen] = dot(ref[...].reshape(slots * blen, cols), weight)
        first += slots * blen


def out_sum(normed, weights, **rest):
    rows = sum(n.shape[0] * n.shape[1] for n in normed)
    return call(
        out_sum_kernel,
        "out_sum",
        [shape_of((rows, weights.shape[1]), F32)],
        [*normed, weights],
        [VMEM] * (len(normed) + 1),
        **rest,
    )[0]


def out_last_kernel(aparts, cap, len_ref, *refs):
    inputs, (w_ref, total_ref, out_ref, held_ref, sem) = refs[:-5], refs[-5:]
    weight = rows_of(w_ref, 0, 1 - core_index(), inputs[0].shape[2])
    lane = lax.axis_index("leaf")
    blen = inputs[0].shape[1]
    row = lax.broadcasted_iota(jnp.int32, (blen, w_ref.shape[1]), 0)
    copies, place = [], 0
    for ref in inputs:
        count = ref.shape[0]
        rows = slice(place * blen, (place + count) * blen)
        total = total_ref[rows] + dot(ref[...].reshape(count * blen, ref.shape[2]), weight)
        for i in range(count):
            slot = (lane ^ aparts[place // cap]) * cap + place % cap
            part = total[i * blen : (i + 1) * blen]
            held_ref[place] = jnp.where(row < len_ref[slot], part, 0.0).astype(BF16)
            copies.append(pltpu.make_async_copy(held_ref.at[place], out_ref.at[slot], sem.at[place]))
            copies[-1].start()
            place += 1
    for copy in copies:
        copy.wait()


def out_last(lengths, normed, aparts, weights, total, **rest):
    slots, blen = lengths.shape[0], normed[0].shape[1]
    shape = (slots, blen, weights.shape[1])
    return call(
        functools.partial(out_last_kernel, aparts, slots // len(aparts)),
        "out_last",
        [shape_of(shape)],
        [lengths, *normed, weights, total],
        [SMEM] + [VMEM] * (2 + len(normed)),
        [ANY],
        scratch=[pltpu.VMEM(shape, BF16), pltpu.SemaphoreType.DMA((slots,))],
        **rest,
    )[0]


def shards(
    trunk_tokens, branch_tokens, fork_offset, fork_tree, branch_len, w_query, w_key, w_value, w_out
):
    lanes, count = lax.axis_size("leaf"), lax.axis_size("trunk")
    bits = [1 << i for i in range(1, count.bit_length() - 1)]
    paired = len(bits) == 2 and lanes % 2 == 0 and (2 * w_key.shape[0]) % DH == 0
    order = []
    chain = functools.partial(touch, order=order)

    if paired:
        kv, qo = [w_key, w_value], [w_query, w_out]
        kv_other = [swap(w, "trunk", 1, "core") for w in kv]
        half = w_key.shape[1] // 2
        kv = [lax.dynamic_slice_in_dim(w, core_index() * half, half, axis=1) for w in kv]
        chain(kv)
        chosen = [(1, [(0, 0, True), (1, 0, True)])]
        (own_kv,) = chip_halves(kv, kv_other, chosen, order=order, weight=40.0)
        near = send_near(own_kv, bits, "kv")
        qo_other = [swap(w, "trunk", 1, "core") for w in qo]
    own_forks = pack_forks(fork_offset, fork_tree, order=order)
    forks = (own_forks, swap(own_forks, "trunk", 1, "forks"))
    trunk_other = swap(trunk_tokens, "trunk", 1, "tokens")
    branch_other = swap(branch_tokens, "trunk", 1, "tokens")
    trunk = trunk_tokens, trunk_other
    if paired:
        chosen = [
            (2, [(0, "even", True)]),
            (2, [(0, "odd", True)]),
            (1, [(1, 0, True), (1, 0, False)]),
            (2, [(1, 0, True), (1, 1, True), (1, 0, False)]),
        ]
        own_q, other_q, own_o, again_o = chip_halves(qo, qo_other, chosen, order=order, landed=[forks[1]])
        _, near[1] = chain([], through=[near[1]])
        arrays, picks = pair = send_far(near, near[1], bits, "kv")
        at_hand = arrays[:3], [part[:3] for part in picks]
        earlier = trunk_partial(*trunk, at_hand, order=order, landed=[branch_other])
        _, own_q = chain(arrays[3:], through=[own_q])
        near_q = send_near(own_q, bits, "query")
        last = arrays[3:], [[(0, i, steps) for _, i, steps in part[3:]] for part in picks]
    else:
        pair = whole_pair([w_key, w_value], 1, [(0, 0), (1, 0)])
        queries = whole_pair([w_query], 2, [(0, 0), (0, 1)])
        out_full = lax.all_gather(w_out, "trunk", axis=0, tiled=True)
        earlier, last = (), pair

    def scan_round(held, number):
        if paired:
            return [turn(h, 1 + number, bits, "scan") for h in held]
        return [swap(h, "trunk", bits[number]) for h in held]

    mask = bits[1] if paired else 0
    held, first, kept = trunk_states(*trunk, last, mask, 1, earlier, order=order)
    terms = [scan_round(first, 0)]
    if paired:
        _, near_q[1] = chain(near_q[2:], through=[near_q[1]], weight=5.0)
        far_q = turn(near_q[1], 2, bits, "query_far")
        across = [swap(a, "leaf", 1, "query_lane") for a in near_q[1:]]
    for number in range(1, len(bits)):
        held = scan_step(held, terms[-1], bits[0] if paired else 0, order=order)
        terms.append(scan_round(held, number))
    if paired:
        _, far_q = chain([], through=[far_q])
        last_q = swap(far_q, "leaf", 1, "query_lane")
        queries = lane_pieces(near_q, far_q, other_q, [*across, last_q])
    (parts,) = fork_parts(forks, *kept, order=order)
    if paired:
        chain(across, weight=6.0)
    sends = fork_states(
        forks, parts, terms, bits, paired, lanes, order=order, through=[own_o] if paired else []
    )
    far = sorted(range(1, lanes), key=lambda a: a == 1)
    moved = {a: swap(sends[a], "leaf", a, "lane") for a in far}
    received = [sends[0]] + [moved[a] for a in range(1, lanes)]
    if paired:
        held_o = turn(sends[lanes], 1, bits, "out")
        _, again_o = chain([last_q], through=[again_o])
        near_o = [sends[lanes], held_o, turn(again_o, 2, bits, "out")]
    q, intra = branch_parts(
        branch_tokens, branch_other, queries, pair, paired, order=order, weight=20.0
    )
    if paired:
        _, near_o[1] = chain([], through=[held_o])
        far_o = turn(near_o[1], 2, bits, "out_far")
        crossed = swap(near_o[1], "trunk", 1, "out_core")
        late = (0, slice(None), slice(near_o[1].shape[2] // 2, None))
        outs = [*near_o, far_o, crossed], [
            [(0, (0,), 0, 0), (1, (0,), 1, 0), (2, (0,), 2, 0), (2, (1,), 2, 1), (3, (0,), 3, 0)],
            [(0, (1,), 0, 0), (1, (1,), 1, 0), (2, (2,), 2, 0), (4, late, 2, 1), (3, (1,), 3, 0)],
        ]
    aparts = sorted(range(lanes), key=lambda a: a == 2)
    split = [aparts[:-1], aparts[-1:]] if lanes > 1 else [aparts]
    mine, other = [], []
    if paired:
        chain(near_o[2:3], weight=1.0)
    for part in split:
        own, theirs = norm_parts(q, intra, received, part, order=order, weight=4.0 if mine else 0.5)
        mine.append(own)
        other.append(swap(theirs, "trunk", 1, "normed"))
    if paired:
        chain(other[:1])
        out_full = place_rows(
            outs, (w_out.shape[0] * count, w_out.shape[1]), order=order, weight=8.0
        )
    total = out_sum(mine, out_full, order=order)
    return out_last(branch_len, other, aparts, out_full, total, order=order)


def solution(mesh):
    in_specs = (
        P("leaf", "trunk", None),
        P(("leaf", "trunk"), None, None),
        P("leaf", "trunk", None),
        P("leaf", "trunk", None),
        P(("leaf", "trunk")),
        P("trunk", None),
        P("trunk", None),
        P("trunk", None),
        P("trunk", None),
    )
    out_specs = P(("leaf", "trunk"), None, None)
    return jax.shard_map(shards, mesh=mesh, in_specs=in_specs, out_specs=out_specs, check_vma=False)
```
